32 devices in a mesh: grp: 2 (over y), chan: 4 (over z), bl: 2 (over x), dir: 2 (over core).
Axes of the slice: x: 2, y: 2, z: 4, core: 2. Of those that a mesh axis runs over, the one named last changes fastest.
Arguments:
- visibility: bfloat16 [2, 8, 64, 4096], P(None, ('grp', 'chan'), 'bl'), parts along dimension 1, may hold values from -18 to 18
- coherency: bfloat16 [2, 8, 10, 64, 4096], P(None, ('grp', 'chan'), 'dir', 'bl'), parts along dimension 1, may hold values from -6 to 6
- gain_start: float32 [2, 8, 10, 512], P(None, ('grp', 'chan'), 'dir', 'bl'), parts along dimension 1, may hold values from -6 to 6
- dual_start: float32 [2, 8, 10, 512], P(None, ('grp', 'chan'), 'dir', 'bl'), parts along dimension 1, may hold values from -2 to 2
- penalty: float32 [20], P(('grp', 'dir')), parts along dimension 0, may hold values from 30 to 300
- tile_pairs: int32 [128, 2], P(('grp', 'bl')), parts along dimension 0, may hold values from 0 to 7, as said below
- valid_counts: int32 [128], P(('grp', 'bl')), parts along dimension 0, may hold values from 1024 to 4096, as said below
- station_order: int32 [1024], P('grp'), parts along dimension 0, may hold values from 0 to 511, each once
Outputs:
- gain_final: float32 [2, 8, 10, 512], P(None, ('grp', 'chan'), 'dir', 'bl'), parts along dimension 1
- dual_final: float32 [2, 8, 10, 512], P(None, ('grp', 'chan'), 'dir', 'bl'), parts along dimension 1
The draws below stay inside these ranges and needn't reach their ends.
There are 2 independent parts, one for each index of `grp`. The reference program is written for one: setup_inputs(seed, part) draws one part's arguments, and reference() takes and returns one part's arrays. A program takes and returns all parts, laid end to end along the dimension named above; each array names one. Nothing has to cross between parts.
Inputs may be any that keep to these rules, and one draw needn't show every extreme that they name: `tile_pairs`: every ordered pair of tiles is the pair of exactly one block. `valid_counts`: some block has all slots valid.
All inputs are finite; a program needn't handle non-finite values.
Results may differ from the reference program's by a relative error of at most 0.0003.
Values may be sent and summed in bfloat16 or wider, within the bound.
A program may use at most 128 MiB of HBM per device.

```python
import math
import jax
import jax.numpy as jnp
from jax import lax

S = 512
TILE = 64
K = 10
NPOLY = 3
ITERS = 2
CH = 4
NT = 8
NBLK = 64
TT = 4096


def draw_tile_pairs(key, part):
    key = jax.random.fold_in(key, 1)
    order = jax.random.permutation(key, NBLK).astype(jnp.int32)
    return jnp.stack([order // NT, order % NT], axis=1).astype(jnp.int32)


def draw_valid_counts(key, part):
    key = jax.random.fold_in(key, 2)
    counts = jax.random.randint(key, (NBLK,), TT // 4, TT + 1, dtype=jnp.int32)
    full_block = jax.random.randint(jax.random.fold_in(key, 5), (), 0, NBLK, dtype=jnp.int32)
    return jnp.where(jnp.arange(NBLK, dtype=jnp.int32) == full_block, TT, counts).astype(jnp.int32)


def block_scale(own_key, shape, cuts, low, top_value):
    def one(dim, shards_of):
        steps = jax.random.uniform(jax.random.fold_in(jax.random.fold_in(own_key, 6), dim), (shards_of,), jnp.float32, low / len(cuts), top_value / len(cuts))
        return jnp.repeat(jnp.exp(steps), shape[dim] // shards_of).reshape((-1,) + (1,) * (len(shape) - dim - 1))

    gain = one(*cuts[0])
    for cut in cuts[1:]:
        gain = gain * one(*cut)
    return gain


def noise(rng, shape, deviation, reach, pieces=(), kind=jnp.bfloat16):
    entries = jax.random.normal(rng, shape, jnp.float32) * deviation
    if len(pieces) > 0:
        entries = block_scale(rng, shape, pieces, -0.22, 0.18) * entries
    return jnp.clip(entries, min=-reach, max=reach).astype(kind)


def setup_inputs(seed: int = 0, part: int = 0) -> dict:
    arg_keys = jax.random.split(jax.random.key(seed), 9)
    part_keys = jax.random.split(jax.random.fold_in(arg_keys[8], part), 9)
    return {
        "visibility": noise(part_keys[0], (2, CH, NBLK, TT), 3.0, 18.0, ((1, 4), (2, 2))),
        "coherency": noise(part_keys[1], (2, CH, K, NBLK, TT), 1.0, 6.0, ((1, 4), (2, 2), (3, 2))),
        "gain_start": noise(part_keys[2], (2, CH, K, S), 1.0, 6.0, ((1, 4), (2, 2), (3, 2)), jnp.float32),
        "dual_start": noise(part_keys[3], (2, CH, K, S), 0.3, 2.0, ((1, 4), (2, 2), (3, 2)), jnp.float32),
        "penalty": jnp.clip(jnp.exp(math.log(300.0) - 2.3025851 * jax.random.uniform(part_keys[4], (K,), jnp.float32) ** block_scale(part_keys[4], (K,), ((0, 2),), -0.2, 0.2)), 30.0, 300.0),
        "tile_pairs": draw_tile_pairs(jax.random.fold_in(jax.random.fold_in(arg_keys[8], part), 71), part),
        "valid_counts": draw_valid_counts(jax.random.fold_in(jax.random.fold_in(arg_keys[8], part), 71), part),
        "station_order": jax.random.permutation(part_keys[7], S).astype(jnp.int32),
    }


def poly_basis(channels):
    points = (2.0 * jnp.arange(channels, dtype=jnp.float32) + 1.0) / channels - 1.0
    columns = []
    for degree in range(NPOLY):
        column = points ** degree
        for earlier in columns:
            column = column - jnp.sum(earlier * column) * earlier
        column = column / jnp.sqrt(jnp.sum(column * column))
        columns.append(column)
    return jnp.stack(columns, axis=1)

def consensus(values, basis_rows):
    moments = jnp.einsum('fj,cfks->cjks', basis_rows, values, precision=lax.Precision.HIGHEST)
    return jnp.einsum('fj,cjks->cfks', basis_rows, moments, precision=lax.Precision.HIGHEST)

def tile_gains(natural, which):
    shaped = natural.reshape(natural.shape[:-1] + (S // TILE, TILE))
    return jnp.take(shaped, which, axis=-2)

def cross_terms(coherent, col_gains):
    coh_real = coherent[0].astype(jnp.float32)
    coh_imag = coherent[1].astype(jnp.float32)
    gain_real = jnp.tile(col_gains[0], TILE)
    gain_imag = jnp.tile(col_gains[1], TILE)
    return (coh_real * gain_real + coh_imag * gain_imag, coh_imag * gain_real - coh_real * gain_imag)

def block_model(row_gains, cross_real, cross_imag):
    gain_real = jnp.repeat(row_gains[0], TILE, axis=-1)
    gain_imag = jnp.repeat(row_gains[1], TILE, axis=-1)
    model_real = lax.optimization_barrier(jnp.sum(gain_real * cross_real - gain_imag * cross_imag, axis=-3))
    model_imag = lax.optimization_barrier(jnp.sum(gain_real * cross_imag + gain_imag * cross_real, axis=-3))
    return (model_real, model_imag)

def row_totals(values):
    return lax.optimization_barrier(jnp.sum(values.reshape(values.shape[:-1] + (TILE, TILE)), axis=-1))

def station_sums(resid_real, resid_imag, valid, cross_real, cross_imag, rows_tile):
    resid_real = jnp.expand_dims(resid_real, -3)
    resid_imag = jnp.expand_dims(resid_imag, -3)
    numer_real = row_totals(resid_real * cross_real + resid_imag * cross_imag)
    numer_imag = row_totals(resid_imag * cross_real - resid_real * cross_imag)
    weight = row_totals(valid * (cross_real * cross_real + cross_imag * cross_imag))
    stacked = jnp.stack([numer_real, numer_imag, weight])
    onehot = (rows_tile[:, None] == jnp.arange(S // TILE, dtype=jnp.int32)[None, :]).astype(jnp.float32)
    summed = jnp.einsum('...bi,bt->...ti', stacked, onehot, precision=lax.Precision.HIGHEST)
    return summed.reshape(summed.shape[:-2] + (S,))

def valid_slots(tile_pairs, valid_counts):
    flat_index = jnp.arange(TILE * TILE, dtype=jnp.int32)
    inside = flat_index[None, :] < valid_counts[:, None]
    diagonal = (tile_pairs[:, 0] == tile_pairs[:, 1])[:, None] & (flat_index // TILE == flat_index % TILE)[None, :]
    return (inside & jnp.logical_not(diagonal)).astype(jnp.float32)

def reference(visibility, coherency, gain_start, dual_start, penalty, tile_pairs, valid_counts, station_order):
    rows_tile = tile_pairs[:, 0]
    cols_tile = tile_pairs[:, 1]
    valid = valid_slots(tile_pairs, valid_counts)
    position = jnp.zeros((S,), jnp.int32).at[station_order].set(jnp.arange(S, dtype=jnp.int32))
    basis_rows = poly_basis(CH)
    stiffness = penalty[None, :, None]
    vis_moved = jnp.moveaxis(visibility, 1, 0)
    coh_moved = jnp.moveaxis(coherency, 1, 0)
    gain_now = gain_start
    dual_now = dual_start
    center = consensus(gain_now + dual_now, basis_rows)

    def per_channel(items):
        vis_one, coh_one, nat_one = items
        cross_real, cross_imag = cross_terms(coh_one, tile_gains(nat_one, cols_tile))
        model_real, model_imag = block_model(tile_gains(nat_one, rows_tile), cross_real, cross_imag)
        flat_vis = vis_one.astype(jnp.float32)
        resid_real = valid * (flat_vis[0] - model_real)
        resid_imag = valid * (flat_vis[1] - model_imag)
        return station_sums(resid_real, resid_imag, valid, cross_real, cross_imag, rows_tile)
    for iteration in range(ITERS):
        natural = jnp.take(gain_now, position, axis=3)
        sums = lax.map(per_channel, (vis_moved, coh_moved, jnp.moveaxis(natural, 1, 0)))
        terms = jnp.take(jnp.moveaxis(sums, 0, 1), station_order, axis=3)
        target = center - dual_now
        denominator = terms[2] + stiffness
        gain_now = jnp.stack([(terms[0] + gain_now[0] * terms[2] + stiffness * target[0]) / denominator, (terms[1] + gain_now[1] * terms[2] + stiffness * target[1]) / denominator])
        center = consensus(gain_now + dual_now, basis_rows)
        dual_now = dual_now + gain_now - center
    return (gain_now, dual_now)
```

```python
import functools

import jax
import jax.numpy as jnp
import numpy as np
from jax import lax
from jax.experimental import pallas as pl
from jax.experimental.pallas import tpu as pltpu
from jax.sharding import PartitionSpec as P

TILE = 64
NPOLY = 3
ITERS = 2
LANES = 128
PAD = 8
MESH = pl.DeviceIdType.MESH
F32 = jnp.float32
BF16 = jnp.bfloat16


def poly_coefficients(channels):
    points = (2.0 * np.arange(channels) + 1.0) / channels - 1.0
    powers = np.stack([points**d for d in range(NPOLY)], axis=1)
    columns = []
    for degree in range(NPOLY):
        own = np.zeros(NPOLY)
        own[degree] = 1.0
        column = powers[:, degree]
        for earlier, earlier_own in columns:
            dot = np.sum(earlier * column)
            column = column - dot * earlier
            own = own - dot * earlier_own
        norm = np.sqrt(np.sum(column * column))
        columns.append((column / norm, own / norm))
    return [[float(c) for c in own] for _, own in columns]


def basis_at(index, channels, coefficients):
    x = (2 * index + 1).astype(F32) * (1.0 / channels) - 1.0
    return [own[0] + x * (own[1] + x * own[2]) for own in coefficients]


def iota(shape, dim):
    return lax.broadcasted_iota(jnp.int32, shape, dim)


def onehot(mask):
    return jnp.where(mask, 1.0, 0.0).astype(BF16)


def two_pieces(values):
    high = values.astype(BF16)
    low = (values - high.astype(F32)).astype(BF16)
    return high, low


def kernel(
    nchan, nbl, ndir, coefficients,
    coh_hbm, vis_hbm, gain_ref, dual_ref, pen_ref, pairs_ref, cnt_ref, ord_ref,
    gout_ref, dout_ref,
    cohv, visv, gbuf, cbuf, psend, prec, dualp, natscr, dmat, emat, rmat, imat, amask,
    colg, rsplit, rowexp, tbuf, rowtile, coltile, limit,
    lsem, hsend, hrecv, gsend, grecv, csend, crecv, psems, precv,
):
    chan = lax.axis_index("chan")
    mb = lax.axis_index("bl")
    md = lax.axis_index("dir")
    mine = mb * ndir + md
    nown = nbl * ndir
    kl = gain_ref.shape[2]
    n = gain_ref.shape[3]
    stations = nbl * n
    nb = pairs_ref.shape[0]
    slots = TILE * TILE
    half = slots // ndir
    rows_half = half // TILE
    ntile = stations // TILE
    kall = ndir * kl

    def group_peer(offset):
        peer = lax.rem(mine + offset, nown)
        return lax.div(peer, ndir), lax.rem(peer, ndir)

    def chan_peer(offset):
        return lax.rem(chan + offset, nchan)

    def own_half():
        return pl.ds(pl.multiple_of(md * half, half), half)

    local = [
        pltpu.make_async_copy(coh_hbm.at[:, 0, :, :, own_half()], cohv.at[md], lsem.at[0]),
        pltpu.make_async_copy(vis_hbm.at[:, 0, :, own_half()], visv, lsem.at[1]),
    ]
    for copy in local:
        copy.start()

    barrier = pltpu.get_barrier_semaphore()
    for offset in range(1, nown):
        pb, pd = group_peer(offset)
        pl.semaphore_signal(barrier, inc=1, device_id={"bl": pb, "dir": pd}, device_id_type=MESH)
    for offset in range(1, nchan):
        pl.semaphore_signal(
            barrier, inc=1, device_id={"chan": chan_peer(offset)}, device_id_type=MESH
        )

    gbuf[0, mb, md] = jnp.zeros((2, PAD, n), F32)
    dualp[...] = jnp.zeros((2, PAD, n), F32)
    psend[...] = jnp.zeros(psend.shape, F32)
    for c in range(2):
        gbuf[0, mb, md, c, 0:kl, :] = gain_ref[c, 0]
        dualp[c, 0:kl, :] = dual_ref[c, 0]
    gain_now = gbuf[0, mb, md]
    dual_now = dualp[...]
    cbuf[0, chan] = gain_now + dual_now

    pl.semaphore_wait(barrier, nown - 1 + nchan - 1)

    halves = []
    for offset in range(1, ndir):
        peer = lax.rem(md + offset, ndir)
        source = lax.rem(md + ndir - offset, ndir)
        copy = pltpu.make_async_remote_copy(
            src_ref=coh_hbm.at[:, 0, :, :, pl.ds(pl.multiple_of(peer * half, half), half)],
            dst_ref=cohv.at[md],
            send_sem=hsend.at[offset],
            recv_sem=hrecv.at[md],
            device_id={"dir": peer},
            device_id_type=MESH,
        )
        arrival = pltpu.make_async_remote_copy(
            src_ref=coh_hbm.at[:, 0, :, :, pl.ds(pl.multiple_of(peer * half, half), half)],
            dst_ref=cohv.at[source],
            send_sem=hsend.at[offset],
            recv_sem=hrecv.at[source],
            device_id={"dir": peer},
            device_id_type=MESH,
        )
        halves.append((copy, arrival))

    def group_copies(source_of, target, send_sem, recv_sem, phase):
        made = []
        for offset in range(1, nown):
            pb, pd = group_peer(offset)
            sb, sd = group_peer(nown - offset)
            common = dict(
                src_ref=source_of(pb, pd),
                send_sem=send_sem.at[phase, offset],
                device_id={"bl": pb, "dir": pd},
                device_id_type=MESH,
            )
            copy = pltpu.make_async_remote_copy(
                dst_ref=target.at[phase, mb, md], recv_sem=recv_sem.at[phase, mine], **common
            )
            arrival = pltpu.make_async_remote_copy(
                dst_ref=target.at[phase, sb, sd],
                recv_sem=recv_sem.at[phase, sb * ndir + sd],
                **common,
            )
            made.append((copy, arrival))
        return made

    def gain_copies(phase):
        return group_copies(lambda pb, pd: gbuf.at[phase, mb, md], gbuf, gsend, grecv, phase)

    def term_copies(phase):
        return group_copies(lambda pb, pd: psend.at[phase, pb, pd], prec, psems, precv, phase)

    def chan_copies(phase):
        made = []
        for offset in range(1, nchan):
            peer = chan_peer(offset)
            source = chan_peer(nchan - offset)
            common = dict(
                src_ref=cbuf.at[phase, chan],
                send_sem=csend.at[phase, offset],
                device_id={"chan": peer},
                device_id_type=MESH,
            )
            copy = pltpu.make_async_remote_copy(
                dst_ref=cbuf.at[phase, chan], recv_sem=crecv.at[phase, chan], **common
            )
            arrival = pltpu.make_async_remote_copy(
                dst_ref=cbuf.at[phase, source], recv_sem=crecv.at[phase, source], **common
            )
            made.append((copy, arrival))
        return made

    def start(copies):
        for copy, _ in copies:
            copy.start()

    def arrive(copies):
        for _, arrival in copies:
            arrival.wait_recv()

    def finish(copies):
        for copy, _ in copies:
            copy.wait_send()

    everything = []
    gains = gain_copies(0)
    start(gains)
    start(halves)
    sums = chan_copies(0)
    start(sums)
    everything += [gains, halves, sums]

    order = ord_ref[...]
    wide = iota((ntile * LANES, stations), 0)
    dmat[...] = onehot(jnp.bitwise_and(wide, TILE - 1) + (wide // LANES) * TILE == order)
    shape = (2 * LANES, half)
    emat[...] = onehot(
        jnp.bitwise_and(iota(shape, 0), LANES - 1) == md * rows_half + iota(shape, 1) // TILE
    )
    shape = (2 * half, LANES)
    rmat[...] = onehot(jnp.bitwise_and(iota(shape, 0), half - 1) // TILE == iota(shape, 1))
    row_in = jnp.bitwise_and(iota((2 * LANES, stations), 0), LANES - 1)
    imat[...] = onehot(
        (row_in < rows_half) & (row_in + md * rows_half == jnp.bitwise_and(order, TILE - 1))
    )
    amask[...] = jnp.where(order // TILE == pairs_ref[:, 0:1], 1.0, 0.0)
    rowtile[...] = jnp.broadcast_to(pairs_ref[:, 0:1], (nb, LANES))
    coltile[...] = jnp.broadcast_to(pairs_ref[:, 1:2], (nb, LANES))
    square = jnp.where(
        iota((nb, nb), 0) == iota((nb, nb), 1), cnt_ref[...].astype(F32), 0.0
    )
    limit[...] = jnp.broadcast_to(jnp.sum(square, axis=1, keepdims=True), (nb, LANES))

    row_k = iota((PAD, n), 0)
    stiffness = jnp.ones((PAD, n), F32)
    for k in range(kl):
        stiffness = jnp.where(row_k == k, pen_ref[k], stiffness)

    def spread_gains(phase):
        held = jnp.concatenate(
            [
                jnp.concatenate([gbuf[phase, b, d, c] for b in range(nbl)], axis=1)
                for d in range(ndir)
                for c in range(2)
            ],
            axis=0,
        )
        first = held.astype(BF16)
        rest = held - first.astype(F32)
        second = rest.astype(BF16)
        third = (rest - second.astype(F32)).astype(BF16)
        pieces = jnp.concatenate([first, second, third], axis=0)
        found = lax.dot_general(
            pieces, dmat[...], (((1,), (1,)), ((), ())), preferred_element_type=F32
        )
        count = held.shape[0]
        natscr[...] = found[0:count] + found[count : 2 * count] + found[2 * count : 3 * count]

        def one(index, carry):
            group = index // kl
            row = group * PAD + lax.rem(index, kl)
            values = natscr[pl.ds(row, 1), :]
            by_row = jnp.zeros((nb, LANES), F32)
            by_col = jnp.zeros((nb, LANES), F32)
            for t in range(ntile):
                tile = values[:, t * LANES : (t + 1) * LANES]
                by_row = jnp.where(rowtile[...] == t, tile, by_row)
                by_col = jnp.where(coltile[...] == t, tile, by_col)
            colg[index] = by_col
            high, low = two_pieces(by_row)
            at = pl.ds(pl.multiple_of(index * nb, nb), nb)
            rsplit[at, 0:LANES] = high
            rsplit[at, LANES : 2 * LANES] = low
            return carry

        lax.fori_loop(0, 2 * kall, one, 0)

        def expand(step, carry):
            at = pl.ds(pl.multiple_of(step * 2 * LANES, 2 * LANES), 2 * LANES)
            rowexp[:, at] = jnp.dot(rsplit[...], emat[:, at], preferred_element_type=F32)
            return carry

        lax.fori_loop(0, half // (2 * LANES), expand, 0)

    def station_terms(phase):
        def tile_step(step, carry):
            g = step // (nb // 16)
            part = lax.rem(step, nb // 16)
            lanes = pl.ds(pl.multiple_of(g * LANES, LANES), LANES)
            lanes_low = pl.ds(pl.multiple_of(half + g * LANES, LANES), LANES)
            blocks = pl.ds(pl.multiple_of(part * 16, 16), 16)

            def at(index):
                return pl.ds(pl.multiple_of(index * nb + part * 16, 16), 16)

            model_r = jnp.zeros((16, LANES), F32)
            model_i = jnp.zeros((16, LANES), F32)
            cross = []
            for d in range(ndir):
                for k in range(kl):
                    re, im = d * 2 * kl + k, d * 2 * kl + kl + k
                    coh_r = cohv[d, 0, k, blocks, lanes].astype(F32)
                    coh_i = cohv[d, 1, k, blocks, lanes].astype(F32)
                    col_r, col_i = colg[re, blocks, :], colg[im, blocks, :]
                    cr = coh_r * col_r + coh_i * col_i
                    ci = coh_i * col_r - coh_r * col_i
                    row_r, row_i = rowexp[at(re), lanes], rowexp[at(im), lanes]
                    model_r = model_r + (row_r * cr - row_i * ci)
                    model_i = model_i + (row_r * ci + row_i * cr)
                    cross.append((cr, ci))
            slot = md * half + g * LANES + iota((16, LANES), 1)
            same = rowtile[blocks, :] == coltile[blocks, :]
            diagonal = same & (slot // TILE == jnp.bitwise_and(slot, TILE - 1))
            inside = slot.astype(F32) < limit[blocks, :]
            valid = jnp.where(inside & jnp.logical_not(diagonal), 1.0, 0.0)
            res_r = valid * (visv[0, blocks, lanes].astype(F32) - model_r)
            res_i = valid * (visv[1, blocks, lanes].astype(F32) - model_i)
            for index, (cr, ci) in enumerate(cross):
                terms = (
                    res_r * cr + res_i * ci,
                    res_i * cr - res_r * ci,
                    valid * (cr * cr + ci * ci),
                )
                for q, term in enumerate(terms):
                    high, low = two_pieces(term)
                    tbuf[at(q * kall + index), lanes] = high
                    tbuf[at(q * kall + index), lanes_low] = low
            return carry

        lax.fori_loop(0, (half // LANES) * (nb // 16), tile_step, 0)

        def reduce_step(step, carry):
            q = step // ndir
            d = lax.rem(step, ndir)
            at = pl.ds(pl.multiple_of(step * kl * nb, kl * nb), kl * nb)
            by_block = jnp.dot(tbuf[at, :], rmat[...], preferred_element_type=F32)
            high, low = two_pieces(by_block)
            placed = jnp.dot(
                jnp.concatenate([high, low], axis=1), imat[...], preferred_element_type=F32
            )
            kept = placed.reshape(kl, nb, stations) * amask[...][None]
            summed = jnp.sum(kept, axis=1)
            for b in range(nbl):
                psend[phase, b, d, q, 0:kl, :] = summed[:, b * n : (b + 1) * n]
            return carry

        lax.fori_loop(0, 3 * ndir, reduce_step, 0)

    mine_basis = basis_at(chan, nchan, coefficients)

    def center_of(phase):
        total = jnp.zeros((2, PAD, n), F32)
        for offset in range(nchan):
            source = chan_peer(offset)
            theirs = basis_at(source, nchan, coefficients)
            scale = sum(a * b for a, b in zip(mine_basis, theirs))
            total = total + scale * cbuf[phase, source]
        return total

    for iteration in range(ITERS):
        arrive(gains)
        spread_gains(iteration)
        if iteration == 0:
            for copy in local:
                copy.wait()
            arrive(halves)
        station_terms(iteration)
        moved = term_copies(iteration)
        start(moved)
        everything.append(moved)
        arrive(sums)
        center = center_of(iteration)
        if iteration > 0:
            dual_now = dual_now + gain_now - center
        target = center - dual_now
        arrive(moved)
        terms = psend[iteration, mb, md]
        for offset in range(1, nown):
            sb, sd = group_peer(offset)
            terms = terms + prec[iteration, sb, sd]
        weight = terms[2]
        denominator = weight + stiffness
        gain_now = jnp.stack(
            [
                (terms[c] + gain_now[c] * weight + stiffness * target[c]) / denominator
                for c in range(2)
            ]
        )
        cbuf[iteration + 1, chan] = gain_now + dual_now
        if iteration + 1 < ITERS:
            gbuf[iteration + 1, mb, md] = gain_now
            gains = gain_copies(iteration + 1)
            start(gains)
            everything.append(gains)
        sums = chan_copies(iteration + 1)
        start(sums)
        everything.append(sums)
    gout_ref[:, 0, :, :] = gain_now[:, 0:kl, :]
    arrive(sums)
    center = center_of(ITERS)
    dual_now = dual_now + gain_now - center
    dout_ref[:, 0, :, :] = dual_now[:, 0:kl, :]
    for copies in everything:
        finish(copies)


def on_device(
    nchan, nbl, ndir,
    visibility, coherency, gain_start, dual_start, penalty, tile_pairs, valid_counts, station_order,
):
    kl = gain_start.shape[2]
    n = gain_start.shape[3]
    nb = tile_pairs.shape[0]
    stations = nbl * n
    half = TILE * TILE // ndir
    kall = ndir * kl
    ntile = stations // TILE
    nown = nbl * ndir
    vmem = pl.BlockSpec(memory_space=pltpu.VMEM)
    smem = pl.BlockSpec(memory_space=pltpu.SMEM)
    hbm = pl.BlockSpec(memory_space=pl.ANY)
    dma = pltpu.SemaphoreType.DMA
    out = jax.ShapeDtypeStruct(gain_start.shape, F32)
    return pl.pallas_call(
        functools.partial(kernel, nchan, nbl, ndir, poly_coefficients(nchan)),
        out_shape=(out, out),
        in_specs=[hbm, hbm, vmem, vmem, smem, vmem, vmem, vmem],
        out_specs=(vmem, vmem),
        scratch_shapes=[
            pltpu.VMEM((ndir, 2, kl, nb, half), BF16),
            pltpu.VMEM((2, nb, half), BF16),
            pltpu.VMEM((ITERS, nbl, ndir, 2, PAD, n), F32),
            pltpu.VMEM((ITERS + 1, nchan, 2, PAD, n), F32),
            pltpu.VMEM((ITERS, nbl, ndir, 3, PAD, n), F32),
            pltpu.VMEM((ITERS, nbl, ndir, 3, PAD, n), F32),
            pltpu.VMEM((2, PAD, n), F32),
            pltpu.VMEM((ndir * 2 * PAD, ntile * LANES), F32),
            pltpu.VMEM((ntile * LANES, stations), BF16),
            pltpu.VMEM((2 * LANES, half), BF16),
            pltpu.VMEM((2 * half, LANES), BF16),
            pltpu.VMEM((2 * LANES, stations), BF16),
            pltpu.VMEM((nb, stations), F32),
            pltpu.VMEM((2 * kall, nb, LANES), F32),
            pltpu.VMEM((2 * kall * nb, 2 * LANES), BF16),
            pltpu.VMEM((2 * kall * nb, half), F32),
            pltpu.VMEM((3 * kall * nb, 2 * half), BF16),
            pltpu.VMEM((nb, LANES), jnp.int32),
            pltpu.VMEM((nb, LANES), jnp.int32),
            pltpu.VMEM((nb, LANES), F32),
            dma((2,)),
            dma((ndir,)),
            dma((ndir,)),
            dma((ITERS, nown)),
            dma((ITERS, nown)),
            dma((ITERS + 1, nchan)),
            dma((ITERS + 1, nchan)),
            dma((ITERS, nown)),
            dma((ITERS, nown)),
        ],
        compiler_params=pltpu.CompilerParams(
            collective_id=0, has_side_effects=True, vmem_limit_bytes=48 * 1024 * 1024
        ),
    )(
        coherency,
        visibility,
        gain_start,
        dual_start,
        penalty,
        tile_pairs,
        valid_counts.reshape(1, nb),
        station_order.reshape(1, stations),
    )


def solution(mesh):
    sizes = mesh.shape
    return jax.shard_map(
        functools.partial(on_device, sizes["chan"], sizes["bl"], sizes["dir"]),
        mesh=mesh,
        in_specs=(
            P(None, ("grp", "chan"), "bl", None),
            P(None, ("grp", "chan"), "dir", "bl", None),
            P(None, ("grp", "chan"), "dir", "bl"),
            P(None, ("grp", "chan"), "dir", "bl"),
            P(("grp", "dir")),
            P(("grp", "bl"), None),
            P(("grp", "bl")),
            P("grp"),
        ),
        out_specs=(P(None, ("grp", "chan"), "dir", "bl"), P(None, ("grp", "chan"), "dir", "bl")),
        check_vma=False,
    )
```

```python
import functools

import jax
import jax.numpy as jnp
import numpy as np
from jax import lax
from jax.experimental import pallas as pl
from jax.experimental.pallas import tpu as pltpu
from jax.sharding import PartitionSpec as P

TILE = 64
NPOLY = 3
ITERS = 2
LANES = 128
PAD = 8
FOLD = 4
GROUP = FOLD * LANES
MESH = pl.DeviceIdType.MESH
F32 = jnp.float32
BF16 = jnp.bfloat16


def poly_coefficients(channels):
    points = (2.0 * np.arange(channels) + 1.0) / channels - 1.0
    powers = np.stack([points**d for d in range(NPOLY)], axis=1)
    columns = []
    for degree in range(NPOLY):
        own = np.zeros(NPOLY)
        own[degree] = 1.0
        column = powers[:, degree]
        for earlier, earlier_own in columns:
            dot = np.sum(earlier * column)
            column = column - dot * earlier
            own = own - dot * earlier_own
        norm = np.sqrt(np.sum(column * column))
        columns.append((column / norm, own / norm))
    return [[float(c) for c in own] for _, own in columns]


def basis_at(index, channels, coefficients):
    x = (2 * index + 1).astype(F32) * (1.0 / channels) - 1.0
    return [own[0] + x * (own[1] + x * own[2]) for own in coefficients]


def iota(shape, dim):
    return lax.broadcasted_iota(jnp.int32, shape, dim)


def onehot(mask):
    return jnp.where(mask, 1.0, 0.0).astype(BF16)


def two_pieces(values):
    high = values.astype(BF16)
    low = (values - high.astype(F32)).astype(BF16)
    return high, low


def kernel(
    nchan, nbl, ndir, coefficients,
    coh_hbm, vis_hbm, gain_hbm, dual_hbm, pen_ref, pairs_hbm, cnt_hbm, ord_hbm,
    gout_ref, dout_ref,
    cohv, visv, cohp, visp, gain_ref, dual_ref, pairs_ref, cnt_ref, ord_ref,
    gbuf, cbuf, psend, prec, dualp, natscr, dmat, perm, rowmat, colmat, rmat, imat, amask,
    rsplit, csplit, rowexp, colexp, tbuf, rowtile, coltile, limit,
    lsem, hsend, hrecv, gsend, grecv, csend, crecv, psems, precv,
):
    chan = lax.axis_index("chan")
    mb = lax.axis_index("bl")
    md = lax.axis_index("dir")
    mine = mb * ndir + md
    nown = nbl * ndir
    kl = gain_hbm.shape[1]
    n = gain_hbm.shape[3]
    stations = nbl * n
    nb = pairs_hbm.shape[1]
    slots = TILE * TILE
    half = slots // ndir
    rows_half = half // TILE
    ntile = stations // TILE
    kall = ndir * kl
    ngroup = half // GROUP
    rows_group = LANES * FOLD // TILE
    per_row = LANES // rows_group

    def group_peer(offset):
        peer = lax.rem(mine + offset, nown)
        return lax.div(peer, ndir), lax.rem(peer, ndir)

    def chan_peer(offset):
        return lax.rem(chan + offset, nchan)

    def own_half():
        return pl.ds(pl.multiple_of(md * half, half), half)

    small = [
        pltpu.make_async_copy(source, target, lsem.at[2 + index])
        for index, (source, target) in enumerate(
            [
                (gain_hbm, gain_ref),
                (dual_hbm, dual_ref),
                (pairs_hbm, pairs_ref),
                (cnt_hbm, cnt_ref),
                (ord_hbm, ord_ref),
            ]
        )
    ]
    local = [
        pltpu.make_async_copy(coh_hbm.at[:, 0, :, :, own_half()], cohv.at[md], lsem.at[0]),
        pltpu.make_async_copy(vis_hbm.at[:, 0, :, own_half()], visv, lsem.at[1]),
    ]
    for copy in small + local:
        copy.start()

    barrier = pltpu.get_barrier_semaphore()
    for offset in range(1, nown):
        pb, pd = group_peer(offset)
        pl.semaphore_signal(barrier, inc=1, device_id={"bl": pb, "dir": pd}, device_id_type=MESH)
    for offset in range(1, nchan):
        pl.semaphore_signal(
            barrier, inc=1, device_id={"chan": chan_peer(offset)}, device_id_type=MESH
        )

    gbuf[0, mb, md] = jnp.zeros((2, PAD, n), F32)
    dualp[...] = jnp.zeros((2, PAD, n), F32)
    psend[...] = jnp.zeros(psend.shape, F32)
    for copy in small:
        copy.wait()
    for c in range(2):
        for k in range(kl):
            gbuf[0, mb, md, c, k : k + 1, :] = gain_ref[c, k]
            dualp[c, k : k + 1, :] = dual_ref[c, k]
    gain_now = gbuf[0, mb, md]
    dual_now = dualp[...]
    cbuf[0, chan] = gain_now + dual_now

    pl.semaphore_wait(barrier, nown - 1 + nchan - 1)

    halves = []
    for offset in range(1, ndir):
        peer = lax.rem(md + offset, ndir)
        source = lax.rem(md + ndir - offset, ndir)
        copy = pltpu.make_async_remote_copy(
            src_ref=coh_hbm.at[:, 0, :, :, pl.ds(pl.multiple_of(peer * half, half), half)],
            dst_ref=cohv.at[md],
            send_sem=hsend.at[offset],
            recv_sem=hrecv.at[md],
            device_id={"dir": peer},
            device_id_type=MESH,
        )
        arrival = pltpu.make_async_remote_copy(
            src_ref=coh_hbm.at[:, 0, :, :, pl.ds(pl.multiple_of(peer * half, half), half)],
            dst_ref=cohv.at[source],
            send_sem=hsend.at[offset],
            recv_sem=hrecv.at[source],
            device_id={"dir": peer},
            device_id_type=MESH,
        )
        halves.append((copy, arrival))

    def group_copies(source_of, target, send_sem, recv_sem, phase):
        made = []
        for offset in range(1, nown):
            pb, pd = group_peer(offset)
            sb, sd = group_peer(nown - offset)
            common = dict(
                src_ref=source_of(pb, pd),
                send_sem=send_sem.at[phase, offset],
                device_id={"bl": pb, "dir": pd},
                device_id_type=MESH,
            )
            copy = pltpu.make_async_remote_copy(
                dst_ref=target.at[phase, mb, md], recv_sem=recv_sem.at[phase, mine], **common
            )
            arrival = pltpu.make_async_remote_copy(
                dst_ref=target.at[phase, sb, sd],
                recv_sem=recv_sem.at[phase, sb * ndir + sd],
                **common,
            )
            made.append((copy, arrival))
        return made

    def gain_copies(phase):
        return group_copies(lambda pb, pd: gbuf.at[phase, mb, md], gbuf, gsend, grecv, phase)

    def term_copies(phase):
        return group_copies(lambda pb, pd: psend.at[phase, pb, pd], prec, psems, precv, phase)

    def chan_copies(phase):
        made = []
        for offset in range(1, nchan):
            peer = chan_peer(offset)
            source = chan_peer(nchan - offset)
            common = dict(
                src_ref=cbuf.at[phase, chan],
                send_sem=csend.at[phase, offset],
                device_id={"chan": peer},
                device_id_type=MESH,
            )
            copy = pltpu.make_async_remote_copy(
                dst_ref=cbuf.at[phase, chan], recv_sem=crecv.at[phase, chan], **common
            )
            arrival = pltpu.make_async_remote_copy(
                dst_ref=cbuf.at[phase, source], recv_sem=crecv.at[phase, source], **common
            )
            made.append((copy, arrival))
        return made

    def start(copies):
        for copy, _ in copies:
            copy.start()

    def arrive(copies):
        for _, arrival in copies:
            arrival.wait_recv()

    def finish(copies):
        for copy, _ in copies:
            copy.wait_send()

    everything = []
    gains = gain_copies(0)
    start(gains)
    start(halves)
    sums = chan_copies(0)
    start(sums)
    everything += [gains, halves, sums]

    order = ord_ref[...]
    wide = iota((ntile * LANES, stations), 0)
    dmat[...] = onehot(jnp.bitwise_and(wide, TILE - 1) + (wide // LANES) * TILE == order)
    shape = (GROUP, GROUP)
    to_lane = jnp.bitwise_and(iota(shape, 1), LANES - 1)
    from_lane = (to_lane // per_row) * TILE + (iota(shape, 1) // LANES) * per_row
    perm[...] = onehot(iota(shape, 0) == from_lane + jnp.bitwise_and(to_lane, per_row - 1))
    shape = (2 * LANES, ngroup * LANES)
    to_lane = iota(shape, 1)
    from_row = jnp.where(
        iota(shape, 0) < 3 * TILE, jnp.bitwise_and(iota(shape, 0), TILE - 1), slots
    )
    rowmat[...] = onehot(from_row == md * rows_half + to_lane // per_row)
    shape = (2 * LANES, GROUP)
    to_lane = iota(shape, 1)
    from_row = jnp.where(
        iota(shape, 0) < 3 * TILE, jnp.bitwise_and(iota(shape, 0), TILE - 1), slots
    )
    colmat[...] = onehot(
        from_row == (to_lane // LANES) * per_row + jnp.bitwise_and(to_lane, per_row - 1)
    )
    shape = (ngroup * LANES, LANES)
    rmat[0 : ngroup * LANES, :] = onehot(iota(shape, 0) // per_row == iota(shape, 1))
    rmat[ngroup * LANES :, :] = onehot(iota(shape, 0) // per_row == iota(shape, 1))
    row_in = jnp.bitwise_and(iota((2 * LANES, stations), 0), LANES - 1)
    imat[...] = onehot(
        (row_in < rows_half) & (row_in + md * rows_half == jnp.bitwise_and(order, TILE - 1))
    )
    def column(row):
        square = jnp.where(iota((nb, nb), 0) == iota((nb, nb), 1), row.astype(F32), 0.0)
        return jnp.sum(square, axis=1, keepdims=True)

    row_column = column(pairs_ref[0:1, :])
    rowtile[...] = jnp.broadcast_to(row_column, (nb, LANES))
    coltile[...] = jnp.broadcast_to(column(pairs_ref[1:2, :]), (nb, LANES))
    limit[...] = jnp.broadcast_to(column(cnt_ref[...]), (nb, LANES))
    amask[...] = jnp.where((order // TILE).astype(F32) == row_column, 1.0, 0.0)

    row_k = iota((PAD, n), 0)
    stiffness = jnp.ones((PAD, n), F32)
    for k in range(kl):
        stiffness = jnp.where(row_k == k, pen_ref[k], stiffness)

    def spread_gains(phase):
        held = jnp.concatenate(
            [
                jnp.concatenate([gbuf[phase, b, d, c] for b in range(nbl)], axis=1)
                for d in range(ndir)
                for c in range(2)
            ],
            axis=0,
        )
        first = held.astype(BF16)
        rest = held - first.astype(F32)
        second = rest.astype(BF16)
        third = (rest - second.astype(F32)).astype(BF16)
        pieces = jnp.concatenate([first, second, third], axis=0)
        found = lax.dot_general(
            pieces, dmat[...], (((1,), (1,)), ((), ())), preferred_element_type=F32
        )
        count = held.shape[0]
        natscr[...] = found[0:count] + found[count : 2 * count] + found[2 * count : 3 * count]

        def one(index, carry):
            group = index // kl
            row = group * PAD + lax.rem(index, kl)
            values = natscr[pl.ds(row, 1), :]
            by_row = jnp.zeros((nb, LANES), F32)
            by_col = jnp.zeros((nb, LANES), F32)
            for t in range(ntile):
                tile = values[:, t * LANES : (t + 1) * LANES]
                by_row = jnp.where(rowtile[...] == float(t), tile, by_row)
                by_col = jnp.where(coltile[...] == float(t), tile, by_col)
            at = pl.ds(pl.multiple_of(index * nb, nb), nb)
            low_lanes = iota((nb, LANES), 1) < TILE
            for gains_of, split in ((by_row, rsplit), (by_col, csplit)):
                first, rest = two_pieces(gains_of)
                rest = gains_of - first.astype(F32)
                second, third = two_pieces(rest)
                split[at, 0:LANES] = jnp.where(
                    low_lanes, first.astype(F32), second.astype(F32)
                ).astype(BF16)
                split[at, LANES : 2 * LANES] = third
            return carry

        lax.fori_loop(0, 2 * kall, one, 0)
        rowexp[...] = jnp.dot(rsplit[...], rowmat[...], preferred_element_type=F32)
        colexp[...] = jnp.dot(csplit[...], colmat[...], preferred_element_type=F32)

    def permute_half(d):
        def step(g, carry):
            lanes = pl.ds(pl.multiple_of(g * GROUP, GROUP), GROUP)
            source = cohv[d, :, :, :, lanes].reshape(2 * kl * nb, GROUP)
            moved = jnp.dot(source, perm[...], preferred_element_type=F32)
            cohp[d, :, :, :, lanes] = moved.reshape(2, kl, nb, GROUP)
            return carry

        lax.fori_loop(0, ngroup, step, 0)

    def permute_vis():
        def step(g, carry):
            lanes = pl.ds(pl.multiple_of(g * GROUP, GROUP), GROUP)
            source = visv[:, :, lanes].reshape(2 * nb, GROUP)
            moved = jnp.dot(source, perm[...], preferred_element_type=F32)
            visp[:, :, lanes] = moved.reshape(2, nb, GROUP)
            return carry

        lax.fori_loop(0, ngroup, step, 0)

    def station_terms(phase):
        def tile_step(step, carry):
            g = step // (nb // PAD)
            part = lax.rem(step, nb // PAD)
            lanes = pl.ds(pl.multiple_of(g * LANES, LANES), LANES)
            blocks = pl.ds(pl.multiple_of(part * PAD, PAD), PAD)

            def at(index):
                return pl.ds(pl.multiple_of(index * nb + part * PAD, PAD), PAD)

            lane = iota((PAD, LANES), 1)
            row = md * rows_half + g * rows_group + lane // per_row
            same = rowtile[blocks, :] == coltile[blocks, :]
            totals = [jnp.zeros((PAD, LANES), F32)] * (3 * kall)
            for v in range(FOLD):
                here = pl.ds(pl.multiple_of(g * GROUP + v * LANES, LANES), LANES)
                cols = slice(v * LANES, (v + 1) * LANES)
                model_r = jnp.zeros((PAD, LANES), F32)
                model_i = jnp.zeros((PAD, LANES), F32)
                cross = []
                for d in range(ndir):
                    for k in range(kl):
                        re, im = d * 2 * kl + k, d * 2 * kl + kl + k
                        coh_r = cohp[d, 0, k, blocks, here]
                        coh_i = cohp[d, 1, k, blocks, here]
                        col_r, col_i = colexp[at(re), cols], colexp[at(im), cols]
                        cr = coh_r * col_r + coh_i * col_i
                        ci = coh_i * col_r - coh_r * col_i
                        row_r, row_i = rowexp[at(re), lanes], rowexp[at(im), lanes]
                        model_r = model_r + (row_r * cr - row_i * ci)
                        model_i = model_i + (row_r * ci + row_i * cr)
                        cross.append((cr, ci))
                col = v * per_row + jnp.bitwise_and(lane, per_row - 1)
                inside = (row * TILE + col).astype(F32) < limit[blocks, :]
                valid = jnp.where(inside & jnp.logical_not(same & (row == col)), 1.0, 0.0)
                res_r = valid * (visp[0, blocks, here] - model_r)
                res_i = valid * (visp[1, blocks, here] - model_i)
                for index, (cr, ci) in enumerate(cross):
                    terms = (
                        res_r * cr + res_i * ci,
                        res_i * cr - res_r * ci,
                        valid * (cr * cr + ci * ci),
                    )
                    for q, term in enumerate(terms):
                        totals[q * kall + index] = totals[q * kall + index] + term
            for index, total in enumerate(totals):
                tbuf[at(index), lanes] = total
            return carry

        lax.fori_loop(0, ngroup * (nb // PAD), tile_step, 0)

        for q in range(3):
            high, low = two_pieces(tbuf[q * kall * nb : (q + 1) * kall * nb, :])
            by_block = jnp.dot(
                jnp.concatenate([high, low], axis=1), rmat[...], preferred_element_type=F32
            )
            high, low = two_pieces(by_block)
            placed = jnp.dot(
                jnp.concatenate([high, low], axis=1), imat[...], preferred_element_type=F32
            )
            kept = placed.reshape(kall, nb, stations) * amask[...][None]
            summed = jnp.sum(kept, axis=1)
            for d in range(ndir):
                for b in range(nbl):
                    psend[phase, b, d, q, 0:kl, :] = summed[
                        d * kl : (d + 1) * kl, b * n : (b + 1) * n
                    ]

    mine_basis = basis_at(chan, nchan, coefficients)

    def center_of(phase):
        total = jnp.zeros((2, PAD, n), F32)
        for offset in range(nchan):
            source = chan_peer(offset)
            theirs = basis_at(source, nchan, coefficients)
            scale = sum(a * b for a, b in zip(mine_basis, theirs))
            total = total + scale * cbuf[phase, source]
        return total

    for iteration in range(ITERS):
        if iteration == 0:
            for copy in local:
                copy.wait()
            permute_half(md)
            permute_vis()
        arrive(gains)
        spread_gains(iteration)
        if iteration == 0:
            arrive(halves)
            for offset in range(1, ndir):
                permute_half(lax.rem(md + offset, ndir))
        station_terms(iteration)
        moved = term_copies(iteration)
        start(moved)
        everything.append(moved)
        arrive(sums)
        center = center_of(iteration)
        if iteration > 0:
            dual_now = dual_now + gain_now - center
        target = center - dual_now
        arrive(moved)
        terms = psend[iteration, mb, md]
        for offset in range(1, nown):
            sb, sd = group_peer(offset)
            terms = terms + prec[iteration, sb, sd]
        weight = terms[2]
        denominator = weight + stiffness
        gain_now = jnp.stack(
            [
                (terms[c] + gain_now[c] * weight + stiffness * target[c]) / denominator
                for c in range(2)
            ]
        )
        cbuf[iteration + 1, chan] = gain_now + dual_now
        if iteration + 1 < ITERS:
            gbuf[iteration + 1, mb, md] = gain_now
            gains = gain_copies(iteration + 1)
            start(gains)
            everything.append(gains)
        sums = chan_copies(iteration + 1)
        start(sums)
        everything.append(sums)
    for c in range(2):
        for k in range(kl):
            gout_ref[c, k] = gain_now[c, k : k + 1, :]
    arrive(sums)
    center = center_of(ITERS)
    dual_now = dual_now + gain_now - center
    for c in range(2):
        for k in range(kl):
            dout_ref[c, k] = dual_now[c, k : k + 1, :]
    for copies in everything:
        finish(copies)


def on_device(
    nchan, nbl, ndir,
    visibility, coherency, gain_start, dual_start, penalty, tile_pairs, valid_counts, station_order,
):
    kl = gain_start.shape[2]
    n = gain_start.shape[3]
    nb = tile_pairs.shape[0]
    stations = nbl * n
    half = TILE * TILE // ndir
    kall = ndir * kl
    ntile = stations // TILE
    nown = nbl * ndir
    vmem = pl.BlockSpec(memory_space=pltpu.VMEM)
    smem = pl.BlockSpec(memory_space=pltpu.SMEM)
    hbm = pl.BlockSpec(memory_space=pl.ANY)
    dma = pltpu.SemaphoreType.DMA
    out = jax.ShapeDtypeStruct((2, kl, 1, n), F32)
    ngroup = half // GROUP
    gain, dual = pl.pallas_call(
        functools.partial(kernel, nchan, nbl, ndir, poly_coefficients(nchan)),
        out_shape=(out, out),
        in_specs=[hbm, hbm, hbm, hbm, smem, hbm, hbm, hbm],
        out_specs=(vmem, vmem),
        scratch_shapes=[
            pltpu.VMEM((ndir, 2, kl, nb, half), BF16),
            pltpu.VMEM((2, nb, half), BF16),
            pltpu.VMEM((ndir, 2, kl, nb, half), F32),
            pltpu.VMEM((2, nb, half), F32),
            pltpu.VMEM((2, kl, 1, n), F32),
            pltpu.VMEM((2, kl, 1, n), F32),
            pltpu.VMEM((2, nb), jnp.int32),
            pltpu.VMEM((1, nb), jnp.int32),
            pltpu.VMEM((1, stations), jnp.int32),
            pltpu.VMEM((ITERS, nbl, ndir, 2, PAD, n), F32),
            pltpu.VMEM((ITERS + 1, nchan, 2, PAD, n), F32),
            pltpu.VMEM((ITERS, nbl, ndir, 3, PAD, n), F32),
            pltpu.VMEM((ITERS, nbl, ndir, 3, PAD, n), F32),
            pltpu.VMEM((2, PAD, n), F32),
            pltpu.VMEM((ndir * 2 * PAD, ntile * LANES), F32),
            pltpu.VMEM((ntile * LANES, stations), BF16),
            pltpu.VMEM((GROUP, GROUP), BF16),
            pltpu.VMEM((2 * LANES, ngroup * LANES), BF16),
            pltpu.VMEM((2 * LANES, GROUP), BF16),
            pltpu.VMEM((2 * ngroup * LANES, LANES), BF16),
            pltpu.VMEM((2 * LANES, stations), BF16),
            pltpu.VMEM((nb, stations), F32),
            pltpu.VMEM((2 * kall * nb, 2 * LANES), BF16),
            pltpu.VMEM((2 * kall * nb, 2 * LANES), BF16),
            pltpu.VMEM((2 * kall * nb, ngroup * LANES), F32),
            pltpu.VMEM((2 * kall * nb, GROUP), F32),
            pltpu.VMEM((3 * kall * nb, ngroup * LANES), F32),
            pltpu.VMEM((nb, LANES), F32),
            pltpu.VMEM((nb, LANES), F32),
            pltpu.VMEM((nb, LANES), F32),
            dma((7,)),
            dma((ndir,)),
            dma((ndir,)),
            dma((ITERS, nown)),
            dma((ITERS, nown)),
            dma((ITERS + 1, nchan)),
            dma((ITERS + 1, nchan)),
            dma((ITERS, nown)),
            dma((ITERS, nown)),
        ],
        compiler_params=pltpu.CompilerParams(
            collective_id=0, has_side_effects=True, vmem_limit_bytes=60 * 1024 * 1024
        ),
    )(
        coherency,
        visibility,
        jnp.transpose(gain_start, (0, 2, 1, 3)),
        jnp.transpose(dual_start, (0, 2, 1, 3)),
        penalty,
        tile_pairs.T,
        valid_counts.reshape(1, nb),
        station_order.reshape(1, stations),
    )
    return jnp.transpose(gain, (0, 2, 1, 3)), jnp.transpose(dual, (0, 2, 1, 3))


def solution(mesh):
    sizes = mesh.shape
    return jax.shard_map(
        functools.partial(on_device, sizes["chan"], sizes["bl"], sizes["dir"]),
        mesh=mesh,
        in_specs=(
            P(None, ("grp", "chan"), "bl", None),
            P(None, ("grp", "chan"), "dir", "bl", None),
            P(None, ("grp", "chan"), "dir", "bl"),
            P(None, ("grp", "chan"), "dir", "bl"),
            P(("grp", "dir")),
            P(("grp", "bl"), None),
            P(("grp", "bl")),
            P("grp"),
        ),
        out_specs=(P(None, ("grp", "chan"), "dir", "bl"), P(None, ("grp", "chan"), "dir", "bl")),
        check_vma=False,
    )
```

```python
import functools

import jax
import jax.numpy as jnp
import numpy as np
from jax import lax
from jax.experimental import pallas as pl
from jax.experimental.pallas import tpu as pltpu
from jax.sharding import PartitionSpec as P

TILE = 64
NPOLY = 3
ITERS = 2
LANES = 128
PAD = 8
FOLD = 4
GROUP = FOLD * LANES
MESH = pl.DeviceIdType.MESH
F32 = jnp.float32
BF16 = jnp.bfloat16


def poly_coefficients(channels):
    points = (2.0 * np.arange(channels) + 1.0) / channels - 1.0
    powers = np.stack([points**d for d in range(NPOLY)], axis=1)
    columns = []
    for degree in range(NPOLY):
        own = np.zeros(NPOLY)
        own[degree] = 1.0
        column = powers[:, degree]
        for earlier, earlier_own in columns:
            dot = np.sum(earlier * column)
            column = column - dot * earlier
            own = own - dot * earlier_own
        norm = np.sqrt(np.sum(column * column))
        columns.append((column / norm, own / norm))
    return [[float(c) for c in own] for _, own in columns]


def basis_at(index, channels, coefficients):
    x = (2 * index + 1).astype(F32) * (1.0 / channels) - 1.0
    return [own[0] + x * (own[1] + x * own[2]) for own in coefficients]


def iota(shape, dim):
    return lax.broadcasted_iota(jnp.int32, shape, dim)


def shift_of(size):
    return jnp.int32(size.bit_length() - 1)


def onehot(mask):
    return jnp.where(mask, 1.0, 0.0).astype(BF16)


def two_pieces(values):
    high = values.astype(BF16)
    low = (values - high.astype(F32)).astype(BF16)
    return high, low


def kernel(
    nchan, nbl, ndir, coefficients,
    coh_hbm, vis_hbm, gain_hbm, dual_hbm, pen_ref, pairs_hbm, cnt_hbm, ord_hbm,
    gout_ref, dout_ref,
    cohv, visv, cohp, visp, gain_ref, dual_ref, pairs_ref, cnt_ref, ord_ref,
    gbuf, cbuf, psend, prec, dualp, perm, rowmat, colmat, rmat, imat, amask,
    tilemask, inmat, select, rowexp, colexp, tbuf, rowtile, coltile, limit,
    lsem, hsend, hrecv, gsend, grecv, csend, crecv, psems, precv,
):
    chan = lax.axis_index("chan")
    mb = lax.axis_index("bl")
    md = lax.axis_index("dir")
    mine = mb * ndir + md
    nown = nbl * ndir
    kl = gain_hbm.shape[1]
    n = gain_hbm.shape[3]
    stations = nbl * n
    nb = pairs_hbm.shape[1]
    slots = TILE * TILE
    half = slots // ndir
    rows_half = half // TILE
    assert stations // TILE <= PAD
    kall = ndir * kl
    ngroup = half // GROUP
    rows_group = LANES * FOLD // TILE
    per_row = LANES // rows_group

    def group_peer(offset):
        peer = lax.rem(mine + offset, nown)
        return lax.div(peer, ndir), lax.rem(peer, ndir)

    def chan_peer(offset):
        return lax.rem(chan + offset, nchan)

    def own_half():
        return pl.ds(pl.multiple_of(md * half, half), half)

    small = [
        pltpu.make_async_copy(source, target, lsem.at[2 + index])
        for index, (source, target) in enumerate(
            [
                (gain_hbm, gain_ref),
                (dual_hbm, dual_ref),
                (pairs_hbm, pairs_ref),
                (cnt_hbm, cnt_ref),
                (ord_hbm, ord_ref),
            ]
        )
    ]
    local = [
        pltpu.make_async_copy(coh_hbm.at[:, 0, :, :, own_half()], cohv.at[md], lsem.at[0]),
        pltpu.make_async_copy(vis_hbm.at[:, 0, :, own_half()], visv, lsem.at[1]),
    ]
    for copy in small + local:
        copy.start()

    barrier = pltpu.get_barrier_semaphore()
    for offset in range(1, nown):
        pb, pd = group_peer(offset)
        pl.semaphore_signal(barrier, inc=1, device_id={"bl": pb, "dir": pd}, device_id_type=MESH)
    for offset in range(1, nchan):
        pl.semaphore_signal(
            barrier, inc=1, device_id={"chan": chan_peer(offset)}, device_id_type=MESH
        )

    gbuf[0, mb, md] = jnp.zeros((2, PAD, n), F32)
    dualp[...] = jnp.zeros((2, PAD, n), F32)
    psend[...] = jnp.zeros(psend.shape, F32)
    for copy in small:
        copy.wait()
    for c in range(2):
        for k in range(kl):
            gbuf[0, mb, md, c, k : k + 1, :] = gain_ref[c, k]
            dualp[c, k : k + 1, :] = dual_ref[c, k]
    gain_now = gbuf[0, mb, md]
    dual_now = dualp[...]
    cbuf[0, chan] = gain_now + dual_now

    pl.semaphore_wait(barrier, nown - 1 + nchan - 1)

    halves = []
    for offset in range(1, ndir):
        peer = lax.rem(md + offset, ndir)
        source = lax.rem(md + ndir - offset, ndir)
        copy = pltpu.make_async_remote_copy(
            src_ref=coh_hbm.at[:, 0, :, :, pl.ds(pl.multiple_of(peer * half, half), half)],
            dst_ref=cohv.at[md],
            send_sem=hsend.at[offset],
            recv_sem=hrecv.at[md],
            device_id={"dir": peer},
            device_id_type=MESH,
        )
        arrival = pltpu.make_async_remote_copy(
            src_ref=coh_hbm.at[:, 0, :, :, pl.ds(pl.multiple_of(peer * half, half), half)],
            dst_ref=cohv.at[source],
            send_sem=hsend.at[offset],
            recv_sem=hrecv.at[source],
            device_id={"dir": peer},
            device_id_type=MESH,
        )
        halves.append((copy, arrival))

    def group_copies(source_of, target, send_sem, recv_sem, phase):
        made = []
        for offset in range(1, nown):
            pb, pd = group_peer(offset)
            sb, sd = group_peer(nown - offset)
            common = dict(
                src_ref=source_of(pb, pd),
                send_sem=send_sem.at[phase, offset],
                device_id={"bl": pb, "dir": pd},
                device_id_type=MESH,
            )
            copy = pltpu.make_async_remote_copy(
                dst_ref=target.at[phase, mb, md], recv_sem=recv_sem.at[phase, mine], **common
            )
            arrival = pltpu.make_async_remote_copy(
                dst_ref=target.at[phase, sb, sd],
                recv_sem=recv_sem.at[phase, sb * ndir + sd],
                **common,
            )
            made.append((copy, arrival))
        return made

    def gain_copies(phase):
        return group_copies(lambda pb, pd: gbuf.at[phase, mb, md], gbuf, gsend, grecv, phase)

    def term_copies(phase):
        return group_copies(lambda pb, pd: psend.at[phase, pb, pd], prec, psems, precv, phase)

    def chan_copies(phase):
        made = []
        for offset in range(1, nchan):
            peer = chan_peer(offset)
            source = chan_peer(nchan - offset)
            common = dict(
                src_ref=cbuf.at[phase, chan],
                send_sem=csend.at[phase, offset],
                device_id={"chan": peer},
                device_id_type=MESH,
            )
            copy = pltpu.make_async_remote_copy(
                dst_ref=cbuf.at[phase, chan], recv_sem=crecv.at[phase, chan], **common
            )
            arrival = pltpu.make_async_remote_copy(
                dst_ref=cbuf.at[phase, source], recv_sem=crecv.at[phase, source], **common
            )
            made.append((copy, arrival))
        return made

    def start(copies):
        for copy, _ in copies:
            copy.start()

    def arrive(copies):
        for _, arrival in copies:
            arrival.wait_recv()

    def finish(copies):
        for copy, _ in copies:
            copy.wait_send()

    everything = []
    gains = gain_copies(0)
    start(gains)
    start(halves)
    sums = chan_copies(0)
    start(sums)
    everything += [gains, halves, sums]

    order = ord_ref[...]
    within = jnp.bitwise_and(order, TILE - 1)
    tile_of = lax.shift_right_logical(order, shift_of(TILE))
    tilemask[...] = jnp.where(iota((PAD, stations), 0) == tile_of, 1.0, 0.0)
    both = iota((LANES, stations), 0)
    inmat[:, 0:stations] = onehot(both == within)
    inmat[:, stations : 2 * stations] = onehot(both - TILE == within)
    to_lane = iota((1, GROUP), 1)
    lane_row = lax.shift_right_logical(jnp.bitwise_and(to_lane, LANES - 1), shift_of(per_row))
    lane_col = lax.shift_right_logical(to_lane, shift_of(LANES)) * per_row + jnp.bitwise_and(
        to_lane, per_row - 1
    )
    perm[...] = onehot(iota((GROUP, GROUP), 0) == lane_row * TILE + lane_col)
    piece_row = jnp.bitwise_and(iota((LANES, GROUP), 0), TILE - 1)
    colmat[...] = onehot(piece_row == lane_col)
    shape = (LANES, ngroup * LANES)
    lane_row = lax.shift_right_logical(iota((1, ngroup * LANES), 1), shift_of(per_row))
    piece_row = jnp.bitwise_and(iota(shape, 0), TILE - 1)
    rowmat[...] = onehot(piece_row == md * rows_half + lane_row)
    shape = (ngroup * LANES, LANES)
    summing = onehot(lax.shift_right_logical(iota(shape, 0), shift_of(per_row)) == iota(shape, 1))
    rmat[0 : ngroup * LANES, :] = summing
    rmat[ngroup * LANES :, :] = summing
    row_in = iota((LANES, stations), 0)
    placing = onehot((row_in < rows_half) & (row_in + md * rows_half == within))
    imat[0:LANES, :] = placing
    imat[LANES : 2 * LANES, :] = placing

    def column(row):
        square = jnp.where(iota((nb, nb), 0) == iota((nb, nb), 1), row.astype(F32), 0.0)
        return jnp.sum(square, axis=1, keepdims=True)

    row_column = column(pairs_ref[0:1, :])
    rowtile[...] = jnp.broadcast_to(row_column, (nb, LANES))
    coltile[...] = jnp.broadcast_to(column(pairs_ref[1:2, :]), (nb, LANES))
    limit[...] = jnp.broadcast_to(column(cnt_ref[...]), (nb, LANES))
    amask[...] = jnp.where(tile_of.astype(F32) == row_column, 1.0, 0.0)
    lane_tile = iota((nb, LANES), 1).astype(F32)
    select[0:nb, :] = onehot(rowtile[...] == lane_tile)
    select[nb : 2 * nb, :] = onehot(coltile[...] == lane_tile)

    row_k = iota((PAD, n), 0)
    stiffness = jnp.ones((PAD, n), F32)
    for k in range(kl):
        stiffness = jnp.where(row_k == k, pen_ref[k], stiffness)

    def spread_gains(phase):
        highs, lows = [], []
        for d in range(ndir):
            for c in range(2):
                held = jnp.concatenate([gbuf[phase, b, d, c] for b in range(nbl)], axis=1)
                first = held.astype(BF16).astype(F32)
                second = held - first
                for k in range(kl):
                    highs.append(first[k : k + 1, :] * tilemask[...])
                    lows.append(second[k : k + 1, :] * tilemask[...])
        pieces = jnp.concatenate(
            [jnp.concatenate(highs, axis=0), jnp.concatenate(lows, axis=0)], axis=1
        ).astype(BF16)
        natural = lax.dot_general(
            pieces, inmat[...], (((1,), (1,)), ((), ())), preferred_element_type=F32
        )
        by_tile = jnp.concatenate(
            [natural[i * PAD : (i + 1) * PAD, :] for i in range(2 * kall)], axis=1
        )
        by_tile = jnp.concatenate([by_tile, jnp.zeros_like(by_tile)], axis=0).astype(BF16)
        chosen = jnp.dot(
            select[:, 0 : 2 * PAD], by_tile, preferred_element_type=F32
        ).astype(BF16)
        for first, table, target in ((0, rowmat, rowexp), (nb, colmat, colexp)):
            stacked = jnp.concatenate(
                [
                    chosen[first : first + nb, i * LANES : (i + 1) * LANES]
                    for i in range(2 * kall)
                ],
                axis=0,
            )
            target[...] = jnp.dot(stacked, table[...], preferred_element_type=F32)

    def permute_half(d):
        def step(g, carry):
            lanes = pl.ds(pl.multiple_of(g * GROUP, GROUP), GROUP)
            source = cohv[d, :, :, :, lanes].reshape(2 * kl * nb, GROUP)
            moved = jnp.dot(source, perm[...], preferred_element_type=F32)
            cohp[d, :, :, :, lanes] = moved.reshape(2, kl, nb, GROUP)
            return carry

        lax.fori_loop(0, ngroup, step, 0)

    def permute_vis():
        def step(g, carry):
            lanes = pl.ds(pl.multiple_of(g * GROUP, GROUP), GROUP)
            source = visv[:, :, lanes].reshape(2 * nb, GROUP)
            moved = jnp.dot(source, perm[...], preferred_element_type=F32)
            visp[:, :, lanes] = moved.reshape(2, nb, GROUP)
            return carry

        lax.fori_loop(0, ngroup, step, 0)

    def station_terms(phase):
        def tile_step(step, carry):
            g = step // (nb // PAD)
            part = lax.rem(step, nb // PAD)
            lanes = pl.ds(pl.multiple_of(g * LANES, LANES), LANES)
            blocks = pl.ds(pl.multiple_of(part * PAD, PAD), PAD)

            def at(index):
                return pl.ds(pl.multiple_of(index * nb + part * PAD, PAD), PAD)

            lane = iota((PAD, LANES), 1)
            row = md * rows_half + g * rows_group + lax.shift_right_logical(lane, shift_of(per_row))
            same = rowtile[blocks, :] == coltile[blocks, :]
            totals = [jnp.zeros((PAD, LANES), F32)] * (3 * kall)
            for v in range(FOLD):
                here = pl.ds(pl.multiple_of(g * GROUP + v * LANES, LANES), LANES)
                cols = slice(v * LANES, (v + 1) * LANES)
                model_r = jnp.zeros((PAD, LANES), F32)
                model_i = jnp.zeros((PAD, LANES), F32)
                cross = []
                for d in range(ndir):
                    for k in range(kl):
                        re, im = d * 2 * kl + k, d * 2 * kl + kl + k
                        coh_r = cohp[d, 0, k, blocks, here]
                        coh_i = cohp[d, 1, k, blocks, here]
                        col_r, col_i = colexp[at(re), cols], colexp[at(im), cols]
                        cr = coh_r * col_r + coh_i * col_i
                        ci = coh_i * col_r - coh_r * col_i
                        row_r, row_i = rowexp[at(re), lanes], rowexp[at(im), lanes]
                        model_r = model_r + (row_r * cr - row_i * ci)
                        model_i = model_i + (row_r * ci + row_i * cr)
                        cross.append((cr, ci))
                col = v * per_row + jnp.bitwise_and(lane, per_row - 1)
                inside = (row * TILE + col).astype(F32) < limit[blocks, :]
                valid = jnp.where(inside & jnp.logical_not(same & (row == col)), 1.0, 0.0)
                res_r = valid * (visp[0, blocks, here] - model_r)
                res_i = valid * (visp[1, blocks, here] - model_i)
                for index, (cr, ci) in enumerate(cross):
                    terms = (
                        res_r * cr + res_i * ci,
                        res_i * cr - res_r * ci,
                        valid * (cr * cr + ci * ci),
                    )
                    for q, term in enumerate(terms):
                        totals[q * kall + index] = totals[q * kall + index] + term
            for index, total in enumerate(totals):
                tbuf[at(index), lanes] = total
            return carry

        lax.fori_loop(0, ngroup * (nb // PAD), tile_step, 0)

        for q in range(3):
            high, low = two_pieces(tbuf[q * kall * nb : (q + 1) * kall * nb, :])
            by_block = jnp.dot(
                jnp.concatenate([high, low], axis=1), rmat[...], preferred_element_type=F32
            )
            high, low = two_pieces(by_block)
            placed = jnp.dot(
                jnp.concatenate([high, low], axis=1), imat[...], preferred_element_type=F32
            )
            kept = placed.reshape(kall, nb, stations) * amask[...][None]
            summed = jnp.sum(kept, axis=1)
            for d in range(ndir):
                for b in range(nbl):
                    psend[phase, b, d, q, 0:kl, :] = summed[
                        d * kl : (d + 1) * kl, b * n : (b + 1) * n
                    ]

    mine_basis = basis_at(chan, nchan, coefficients)

    def center_of(phase):
        total = jnp.zeros((2, PAD, n), F32)
        for offset in range(nchan):
            source = chan_peer(offset)
            theirs = basis_at(source, nchan, coefficients)
            scale = sum(a * b for a, b in zip(mine_basis, theirs))
            total = total + scale * cbuf[phase, source]
        return total

    for iteration in range(ITERS):
        if iteration == 0:
            for copy in local:
                copy.wait()
            permute_half(md)
            permute_vis()
        arrive(gains)
        spread_gains(iteration)
        if iteration == 0:
            arrive(halves)
            for offset in range(1, ndir):
                permute_half(lax.rem(md + offset, ndir))
        station_terms(iteration)
        moved = term_copies(iteration)
        start(moved)
        everything.append(moved)
        arrive(sums)
        center = center_of(iteration)
        if iteration > 0:
            dual_now = dual_now + gain_now - center
        target = center - dual_now
        arrive(moved)
        terms = psend[iteration, mb, md]
        for offset in range(1, nown):
            sb, sd = group_peer(offset)
            terms = terms + prec[iteration, sb, sd]
        weight = terms[2]
        denominator = weight + stiffness
        gain_now = jnp.stack(
            [
                (terms[c] + gain_now[c] * weight + stiffness * target[c]) / denominator
                for c in range(2)
            ]
        )
        cbuf[iteration + 1, chan] = gain_now + dual_now
        if iteration + 1 < ITERS:
            gbuf[iteration + 1, mb, md] = gain_now
            gains = gain_copies(iteration + 1)
            start(gains)
            everything.append(gains)
        sums = chan_copies(iteration + 1)
        start(sums)
        everything.append(sums)
    for c in range(2):
        for k in range(kl):
            gout_ref[c, k] = gain_now[c, k : k + 1, :]
    arrive(sums)
    center = center_of(ITERS)
    dual_now = dual_now + gain_now - center
    for c in range(2):
        for k in range(kl):
            dout_ref[c, k] = dual_now[c, k : k + 1, :]
    for copies in everything:
        finish(copies)


def hand_over(gain_ref, dual_ref, gout_ref, dout_ref):
    gout_ref[...] = gain_ref[...]
    dout_ref[...] = dual_ref[...]


def on_device(
    nchan, nbl, ndir,
    visibility, coherency, gain_start, dual_start, penalty, tile_pairs, valid_counts, station_order,
):
    kl = gain_start.shape[2]
    n = gain_start.shape[3]
    nb = tile_pairs.shape[0]
    stations = nbl * n
    half = TILE * TILE // ndir
    kall = ndir * kl
    nown = nbl * ndir
    vmem = pl.BlockSpec(memory_space=pltpu.VMEM)
    smem = pl.BlockSpec(memory_space=pltpu.SMEM)
    hbm = pl.BlockSpec(memory_space=pl.ANY)
    dma = pltpu.SemaphoreType.DMA
    out = jax.ShapeDtypeStruct((2, kl, 1, n), F32)
    ngroup = half // GROUP
    gain, dual = pl.pallas_call(
        functools.partial(kernel, nchan, nbl, ndir, poly_coefficients(nchan)),
        out_shape=(out, out),
        in_specs=[hbm, hbm, hbm, hbm, smem, hbm, hbm, hbm],
        out_specs=(vmem, vmem),
        scratch_shapes=[
            pltpu.VMEM((ndir, 2, kl, nb, half), BF16),
            pltpu.VMEM((2, nb, half), BF16),
            pltpu.VMEM((ndir, 2, kl, nb, half), F32),
            pltpu.VMEM((2, nb, half), F32),
            pltpu.VMEM((2, kl, 1, n), F32),
            pltpu.VMEM((2, kl, 1, n), F32),
            pltpu.VMEM((2, nb), jnp.int32),
            pltpu.VMEM((1, nb), jnp.int32),
            pltpu.VMEM((1, stations), jnp.int32),
            pltpu.VMEM((ITERS, nbl, ndir, 2, PAD, n), F32),
            pltpu.VMEM((ITERS + 1, nchan, 2, PAD, n), F32),
            pltpu.VMEM((ITERS, nbl, ndir, 3, PAD, n), F32),
            pltpu.VMEM((ITERS, nbl, ndir, 3, PAD, n), F32),
            pltpu.VMEM((2, PAD, n), F32),
            pltpu.VMEM((GROUP, GROUP), BF16),
            pltpu.VMEM((LANES, ngroup * LANES), BF16),
            pltpu.VMEM((LANES, GROUP), BF16),
            pltpu.VMEM((2 * ngroup * LANES, LANES), BF16),
            pltpu.VMEM((2 * LANES, stations), BF16),
            pltpu.VMEM((nb, stations), F32),
            pltpu.VMEM((PAD, stations), F32),
            pltpu.VMEM((LANES, 2 * stations), BF16),
            pltpu.VMEM((2 * nb, LANES), BF16),
            pltpu.VMEM((2 * kall * nb, ngroup * LANES), F32),
            pltpu.VMEM((2 * kall * nb, GROUP), F32),
            pltpu.VMEM((3 * kall * nb, ngroup * LANES), F32),
            pltpu.VMEM((nb, LANES), F32),
            pltpu.VMEM((nb, LANES), F32),
            pltpu.VMEM((nb, LANES), F32),
            dma((7,)),
            dma((ndir,)),
            dma((ndir,)),
            dma((ITERS, nown)),
            dma((ITERS, nown)),
            dma((ITERS + 1, nchan)),
            dma((ITERS + 1, nchan)),
            dma((ITERS, nown)),
            dma((ITERS, nown)),
        ],
        compiler_params=pltpu.CompilerParams(
            collective_id=0, has_side_effects=True, vmem_limit_bytes=60 * 1024 * 1024
        ),
    )(
        coherency,
        visibility,
        jnp.transpose(gain_start, (0, 2, 1, 3)),
        jnp.transpose(dual_start, (0, 2, 1, 3)),
        penalty,
        tile_pairs.T,
        valid_counts.reshape(1, nb),
        station_order.reshape(1, stations),
    )
    gain, dual = pl.pallas_call(
        hand_over, out_shape=(out, out), in_specs=[vmem, vmem], out_specs=(vmem, vmem)
    )(gain, dual)
    return jnp.transpose(gain, (0, 2, 1, 3)), jnp.transpose(dual, (0, 2, 1, 3))


def solution(mesh):
    sizes = mesh.shape
    return jax.shard_map(
        functools.partial(on_device, sizes["chan"], sizes["bl"], sizes["dir"]),
        mesh=mesh,
        in_specs=(
            P(None, ("grp", "chan"), "bl", None),
            P(None, ("grp", "chan"), "dir", "bl", None),
            P(None, ("grp", "chan"), "dir", "bl"),
            P(None, ("grp", "chan"), "dir", "bl"),
            P(("grp", "dir")),
            P(("grp", "bl"), None),
            P(("grp", "bl")),
            P("grp"),
        ),
        out_specs=(P(None, ("grp", "chan"), "dir", "bl"), P(None, ("grp", "chan"), "dir", "bl")),
        check_vma=False,
    )
```

```python
import functools

import jax
import jax.numpy as jnp
import numpy as np
from jax import lax
from jax.experimental import pallas as pl
from jax.experimental.pallas import tpu as pltpu
from jax.sharding import PartitionSpec as P

TILE = 64
NPOLY = 3
ITERS = 2
LANES = 128
PAD = 8
FOLD = 4
GROUP = FOLD * LANES
MESH = pl.DeviceIdType.MESH
F32 = jnp.float32
BF16 = jnp.bfloat16


def poly_coefficients(channels):
    points = (2.0 * np.arange(channels) + 1.0) / channels - 1.0
    powers = np.stack([points**d for d in range(NPOLY)], axis=1)
    columns = []
    for degree in range(NPOLY):
        own = np.zeros(NPOLY)
        own[degree] = 1.0
        column = powers[:, degree]
        for earlier, earlier_own in columns:
            dot = np.sum(earlier * column)
            column = column - dot * earlier
            own = own - dot * earlier_own
        norm = np.sqrt(np.sum(column * column))
        columns.append((column / norm, own / norm))
    return [[float(c) for c in own] for _, own in columns]


def basis_at(index, channels, coefficients):
    x = (2 * index + 1).astype(F32) * (1.0 / channels) - 1.0
    return [own[0] + x * (own[1] + x * own[2]) for own in coefficients]


def iota(shape, dim):
    return lax.broadcasted_iota(jnp.int32, shape, dim)


def shift_of(size):
    return jnp.int32(size.bit_length() - 1)


def onehot(mask):
    return jnp.where(mask, 1.0, 0.0).astype(BF16)


def two_pieces(values):
    high = values.astype(BF16)
    low = (values - high.astype(F32)).astype(BF16)
    return high, low


def kernel(
    nchan, nbl, ndir, coefficients,
    coh_hbm, vis_hbm, gain_hbm, dual_hbm, pen_ref, pairs_hbm, cnt_hbm, ord_hbm,
    gout_ref, dout_ref,
    cohv, visv, cohp, visp, gain_ref, dual_ref, pairs_ref, cnt_ref, ord_ref,
    gbuf, cbuf, psend, prec, dualp, perm, rowmat, colmat, rmat, imat, amask,
    tilemask, inmat, select, rowexp, colexp, cross, tbuf, rowtile, coltile, limit,
    lsem, hsend, hrecv, gsend, grecv, csend, crecv, psems, precv,
):
    chan = lax.axis_index("chan")
    mb = lax.axis_index("bl")
    md = lax.axis_index("dir")
    mine = mb * ndir + md
    nown = nbl * ndir
    kl = gain_hbm.shape[1]
    n = gain_hbm.shape[3]
    stations = nbl * n
    nb = pairs_hbm.shape[1]
    slots = TILE * TILE
    half = slots // ndir
    rows_half = half // TILE
    assert stations // TILE <= PAD
    kall = ndir * kl
    ngroup = half // GROUP
    rows_group = LANES * FOLD // TILE
    per_row = LANES // rows_group

    def group_peer(offset):
        peer = lax.rem(mine + offset, nown)
        return lax.div(peer, ndir), lax.rem(peer, ndir)

    def chan_peer(offset):
        return lax.rem(chan + offset, nchan)

    def own_half():
        return pl.ds(pl.multiple_of(md * half, half), half)

    small = [
        pltpu.make_async_copy(source, target, lsem.at[2 + index])
        for index, (source, target) in enumerate(
            [
                (gain_hbm, gain_ref),
                (dual_hbm, dual_ref),
                (pairs_hbm, pairs_ref),
                (cnt_hbm, cnt_ref),
                (ord_hbm, ord_ref),
            ]
        )
    ]
    local = [
        pltpu.make_async_copy(coh_hbm.at[:, 0, :, :, own_half()], cohv.at[md], lsem.at[0]),
        pltpu.make_async_copy(vis_hbm.at[:, 0, :, own_half()], visv, lsem.at[1]),
    ]
    for copy in small + local:
        copy.start()

    barrier = pltpu.get_barrier_semaphore()
    for offset in range(1, nown):
        pb, pd = group_peer(offset)
        pl.semaphore_signal(barrier, inc=1, device_id={"bl": pb, "dir": pd}, device_id_type=MESH)
    for offset in range(1, nchan):
        pl.semaphore_signal(
            barrier, inc=1, device_id={"chan": chan_peer(offset)}, device_id_type=MESH
        )

    gbuf[0, mb, md] = jnp.zeros((2, PAD, n), F32)
    dualp[...] = jnp.zeros((2, PAD, n), F32)
    psend[...] = jnp.zeros(psend.shape, F32)
    for copy in small:
        copy.wait()
    for c in range(2):
        for k in range(kl):
            gbuf[0, mb, md, c, k : k + 1, :] = gain_ref[c, k]
            dualp[c, k : k + 1, :] = dual_ref[c, k]
    gain_now = gbuf[0, mb, md]
    dual_now = dualp[...]
    cbuf[0, chan] = gain_now + dual_now

    pl.semaphore_wait(barrier, nown - 1 + nchan - 1)

    halves = []
    for offset in range(1, ndir):
        peer = lax.rem(md + offset, ndir)
        source = lax.rem(md + ndir - offset, ndir)
        copy = pltpu.make_async_remote_copy(
            src_ref=coh_hbm.at[:, 0, :, :, pl.ds(pl.multiple_of(peer * half, half), half)],
            dst_ref=cohv.at[md],
            send_sem=hsend.at[offset],
            recv_sem=hrecv.at[md],
            device_id={"dir": peer},
            device_id_type=MESH,
        )
        arrival = pltpu.make_async_remote_copy(
            src_ref=coh_hbm.at[:, 0, :, :, pl.ds(pl.multiple_of(peer * half, half), half)],
            dst_ref=cohv.at[source],
            send_sem=hsend.at[offset],
            recv_sem=hrecv.at[source],
            device_id={"dir": peer},
            device_id_type=MESH,
        )
        halves.append((copy, arrival))

    def group_copies(source_of, target, send_sem, recv_sem, phase):
        made = []
        for offset in range(1, nown):
            pb, pd = group_peer(offset)
            sb, sd = group_peer(nown - offset)
            common = dict(
                src_ref=source_of(pb, pd),
                send_sem=send_sem.at[phase, offset],
                device_id={"bl": pb, "dir": pd},
                device_id_type=MESH,
            )
            copy = pltpu.make_async_remote_copy(
                dst_ref=target.at[phase, mb, md, :, 0:kl, :], recv_sem=recv_sem.at[phase, mine], **common
            )
            arrival = pltpu.make_async_remote_copy(
                dst_ref=target.at[phase, sb, sd, :, 0:kl, :],
                recv_sem=recv_sem.at[phase, sb * ndir + sd],
                **common,
            )
            made.append((copy, arrival))
        return made

    def gain_copies(phase):
        return group_copies(
            lambda pb, pd: gbuf.at[phase, mb, md, :, 0:kl, :], gbuf, gsend, grecv, phase
        )

    def term_copies(phase):
        return group_copies(
            lambda pb, pd: psend.at[phase, pb, pd, :, 0:kl, :], prec, psems, precv, phase
        )

    def chan_copies(phase):
        made = []
        for offset in range(1, nchan):
            peer = chan_peer(offset)
            source = chan_peer(nchan - offset)
            common = dict(
                src_ref=cbuf.at[phase, chan, :, 0:kl, :],
                send_sem=csend.at[phase, offset],
                device_id={"chan": peer},
                device_id_type=MESH,
            )
            copy = pltpu.make_async_remote_copy(
                dst_ref=cbuf.at[phase, chan, :, 0:kl, :], recv_sem=crecv.at[phase, chan], **common
            )
            arrival = pltpu.make_async_remote_copy(
                dst_ref=cbuf.at[phase, source, :, 0:kl, :], recv_sem=crecv.at[phase, source], **common
            )
            made.append((copy, arrival))
        return made

    def start(copies):
        for copy, _ in copies:
            copy.start()

    def arrive(copies):
        for _, arrival in copies:
            arrival.wait_recv()

    def finish(copies):
        for copy, _ in copies:
            copy.wait_send()

    everything = []
    gains = gain_copies(0)
    start(gains)
    start(halves)
    sums = chan_copies(0)
    start(sums)
    everything += [gains, halves, sums]

    order = ord_ref[...]
    within = jnp.bitwise_and(order, TILE - 1)
    tile_of = lax.shift_right_logical(order, shift_of(TILE))
    tilemask[...] = jnp.where(iota((PAD, stations), 0) == tile_of, 1.0, 0.0)
    both = iota((LANES, stations), 0)
    inmat[:, 0:stations] = onehot(both == within)
    inmat[:, stations : 2 * stations] = onehot(both - TILE == within)
    to_lane = iota((1, GROUP), 1)
    lane_row = lax.shift_right_logical(jnp.bitwise_and(to_lane, LANES - 1), shift_of(per_row))
    lane_col = lax.shift_right_logical(to_lane, shift_of(LANES)) * per_row + jnp.bitwise_and(
        to_lane, per_row - 1
    )
    perm[...] = onehot(iota((GROUP, GROUP), 0) == lane_row * TILE + lane_col)
    piece_row = jnp.bitwise_and(iota((LANES, GROUP), 0), TILE - 1)
    colmat[...] = onehot(piece_row == lane_col)
    shape = (LANES, ngroup * LANES)
    lane_row = lax.shift_right_logical(iota((1, ngroup * LANES), 1), shift_of(per_row))
    piece_row = jnp.bitwise_and(iota(shape, 0), TILE - 1)
    rowmat[...] = onehot(piece_row == md * rows_half + lane_row)
    shape = (ngroup * LANES, LANES)
    summing = onehot(lax.shift_right_logical(iota(shape, 0), shift_of(per_row)) == iota(shape, 1))
    rmat[0 : ngroup * LANES, :] = summing
    rmat[ngroup * LANES :, :] = summing
    row_in = iota((LANES, stations), 0)
    placing = onehot((row_in < rows_half) & (row_in + md * rows_half == within))
    imat[0:LANES, :] = placing
    imat[LANES : 2 * LANES, :] = placing

    def column(row):
        square = jnp.where(iota((nb, nb), 0) == iota((nb, nb), 1), row.astype(F32), 0.0)
        return jnp.sum(square, axis=1, keepdims=True)

    row_column = column(pairs_ref[0:1, :])
    rowtile[...] = jnp.broadcast_to(row_column, (nb, LANES))
    coltile[...] = jnp.broadcast_to(column(pairs_ref[1:2, :]), (nb, LANES))
    limit[...] = jnp.broadcast_to(column(cnt_ref[...]), (nb, LANES))
    amask[...] = jnp.where(tile_of.astype(F32) == row_column, 1.0, 0.0)
    lane_tile = iota((nb, LANES), 1).astype(F32)
    select[0:nb, :] = onehot(rowtile[...] == lane_tile)
    select[nb : 2 * nb, :] = onehot(coltile[...] == lane_tile)

    row_k = iota((PAD, n), 0)
    stiffness = jnp.ones((PAD, n), F32)
    for k in range(kl):
        stiffness = jnp.where(row_k == k, pen_ref[k], stiffness)

    def spread_gains(phase):
        highs, lows = [], []
        for d in range(ndir):
            for c in range(2):
                held = jnp.concatenate([gbuf[phase, b, d, c] for b in range(nbl)], axis=1)
                first = held.astype(BF16).astype(F32)
                second = held - first
                for k in range(kl):
                    highs.append(first[k : k + 1, :] * tilemask[...])
                    lows.append(second[k : k + 1, :] * tilemask[...])
        pieces = jnp.concatenate(
            [jnp.concatenate(highs, axis=0), jnp.concatenate(lows, axis=0)], axis=1
        ).astype(BF16)
        natural = lax.dot_general(
            pieces, inmat[...], (((1,), (1,)), ((), ())), preferred_element_type=F32
        )
        by_tile = jnp.concatenate(
            [natural[i * PAD : (i + 1) * PAD, :] for i in range(2 * kall)], axis=1
        )
        by_tile = jnp.concatenate([by_tile, jnp.zeros_like(by_tile)], axis=0).astype(BF16)
        chosen = jnp.dot(
            select[:, 0 : 2 * PAD], by_tile, preferred_element_type=F32
        ).astype(BF16)
        for first, table, target in ((0, rowmat, rowexp), (nb, colmat, colexp)):
            stacked = jnp.concatenate(
                [
                    chosen[first : first + nb, i * LANES : (i + 1) * LANES]
                    for i in range(2 * kall)
                ],
                axis=0,
            )
            target[...] = jnp.dot(stacked, table[...], preferred_element_type=F32)

    def valid_slots(g):
        lane = iota((nb, GROUP), 1)
        in_lane = jnp.bitwise_and(lane, LANES - 1)
        row = md * rows_half + g * rows_group + lax.shift_right_logical(in_lane, shift_of(per_row))
        col = lax.shift_right_logical(lane, shift_of(LANES)) * per_row + jnp.bitwise_and(
            lane, per_row - 1
        )

        def across(table):
            return jnp.concatenate([table[...]] * FOLD, axis=1)

        inside = (row * TILE + col).astype(F32) < across(limit)
        same = across(rowtile) == across(coltile)
        return jnp.where(inside & jnp.logical_not(same & (row == col)), 1.0, 0.0)

    def permute_half(d):
        def step(g, carry):
            lanes = pl.ds(pl.multiple_of(g * GROUP, GROUP), GROUP)
            source = cohv[d, :, :, :, lanes].reshape(2 * kl * nb, GROUP)
            moved = jnp.dot(source, perm[...], preferred_element_type=F32)
            moved = moved.reshape(2, kl, nb, GROUP)
            cohp[d, :, :, :, lanes] = moved * valid_slots(g)[None, None]
            return carry

        lax.fori_loop(0, ngroup, step, 0)

    def permute_vis():
        def step(g, carry):
            lanes = pl.ds(pl.multiple_of(g * GROUP, GROUP), GROUP)
            source = visv[:, :, lanes].reshape(2 * nb, GROUP)
            moved = jnp.dot(source, perm[...], preferred_element_type=F32)
            visp[:, :, lanes] = moved.reshape(2, nb, GROUP)
            return carry

        lax.fori_loop(0, ngroup, step, 0)

    def station_terms(phase):
        def tile_step(step, carry):
            g = step // (nb // PAD)
            part = lax.rem(step, nb // PAD)
            lanes = pl.ds(pl.multiple_of(g * LANES, LANES), LANES)
            blocks = pl.ds(pl.multiple_of(part * PAD, PAD), PAD)

            def at(index):
                return pl.ds(pl.multiple_of(index * nb + part * PAD, PAD), PAD)

            residuals = []
            for v in range(FOLD):
                here = pl.ds(pl.multiple_of(g * GROUP + v * LANES, LANES), LANES)
                cols = slice(v * LANES, (v + 1) * LANES)
                model_r = jnp.zeros((PAD, LANES), F32)
                model_i = jnp.zeros((PAD, LANES), F32)
                for d in range(ndir):
                    for k in range(kl):
                        re, im = d * 2 * kl + k, d * 2 * kl + kl + k
                        coh_r = cohp[d, 0, k, blocks, here]
                        coh_i = cohp[d, 1, k, blocks, here]
                        col_r, col_i = colexp[at(re), cols], colexp[at(im), cols]
                        cr = coh_r * col_r + coh_i * col_i
                        ci = coh_i * col_r - coh_r * col_i
                        cross[d * kl + k, 0, v] = cr
                        cross[d * kl + k, 1, v] = ci
                        row_r, row_i = rowexp[at(re), lanes], rowexp[at(im), lanes]
                        model_r = model_r + (row_r * cr - row_i * ci)
                        model_i = model_i + (row_r * ci + row_i * cr)
                res_r = visp[0, blocks, here] - model_r
                res_i = visp[1, blocks, here] - model_i
                residuals.append((res_r, res_i))
            for index in range(kall):
                numer_r = numer_i = weight = None
                for v, (res_r, res_i) in enumerate(residuals):
                    cr, ci = cross[index, 0, v], cross[index, 1, v]
                    parts = (
                        res_r * cr + res_i * ci,
                        res_i * cr - res_r * ci,
                        cr * cr + ci * ci,
                    )
                    if numer_r is None:
                        numer_r, numer_i, weight = parts
                    else:
                        numer_r = numer_r + parts[0]
                        numer_i = numer_i + parts[1]
                        weight = weight + parts[2]
                tbuf[at(index), lanes] = numer_r
                tbuf[at(kall + index), lanes] = numer_i
                tbuf[at(2 * kall + index), lanes] = weight
            return carry

        lax.fori_loop(0, ngroup * (nb // PAD), tile_step, 0)

        high, low = two_pieces(tbuf[...])
        by_block = jnp.dot(
            jnp.concatenate([high, low], axis=1), rmat[...], preferred_element_type=F32
        )
        high, low = two_pieces(by_block)
        placed = jnp.dot(
            jnp.concatenate([high, low], axis=1), imat[...], preferred_element_type=F32
        )
        kept = placed.reshape(3 * kall, nb, stations) * amask[...][None]
        summed = jnp.sum(kept, axis=1)
        for q in range(3):
            for d in range(ndir):
                at = (q * ndir + d) * kl
                for b in range(nbl):
                    psend[phase, b, d, q, 0:kl, :] = summed[at : at + kl, b * n : (b + 1) * n]

    mine_basis = basis_at(chan, nchan, coefficients)

    def center_of(phase):
        total = jnp.zeros((2, PAD, n), F32)
        for offset in range(nchan):
            source = chan_peer(offset)
            theirs = basis_at(source, nchan, coefficients)
            scale = sum(a * b for a, b in zip(mine_basis, theirs))
            total = total + scale * cbuf[phase, source]
        return total

    for iteration in range(ITERS):
        if iteration == 0:
            for copy in local:
                copy.wait()
            permute_half(md)
            permute_vis()
        arrive(gains)
        spread_gains(iteration)
        if iteration == 0:
            arrive(halves)
            for offset in range(1, ndir):
                permute_half(lax.rem(md + offset, ndir))
        station_terms(iteration)
        moved = term_copies(iteration)
        start(moved)
        everything.append(moved)
        arrive(sums)
        center = center_of(iteration)
        if iteration > 0:
            dual_now = dual_now + gain_now - center
        target = center - dual_now
        arrive(moved)
        terms = psend[iteration, mb, md]
        for offset in range(1, nown):
            sb, sd = group_peer(offset)
            terms = terms + prec[iteration, sb, sd]
        weight = terms[2]
        denominator = weight + stiffness
        gain_now = jnp.stack(
            [
                (terms[c] + gain_now[c] * weight + stiffness * target[c]) / denominator
                for c in range(2)
            ]
        )
        cbuf[iteration + 1, chan] = gain_now + dual_now
        if iteration + 1 < ITERS:
            gbuf[iteration + 1, mb, md] = gain_now
            gains = gain_copies(iteration + 1)
            start(gains)
            everything.append(gains)
        sums = chan_copies(iteration + 1)
        start(sums)
        everything.append(sums)
    for c in range(2):
        for k in range(kl):
            gout_ref[c, k] = gain_now[c, k : k + 1, :]
    arrive(sums)
    center = center_of(ITERS)
    dual_now = dual_now + gain_now - center
    for c in range(2):
        for k in range(kl):
            dout_ref[c, k] = dual_now[c, k : k + 1, :]
    for copies in everything:
        finish(copies)


def hand_over(gain_ref, dual_ref, gout_ref, dout_ref):
    gout_ref[...] = gain_ref[...]
    dout_ref[...] = dual_ref[...]


def on_device(
    nchan, nbl, ndir,
    visibility, coherency, gain_start, dual_start, penalty, tile_pairs, valid_counts, station_order,
):
    kl = gain_start.shape[2]
    n = gain_start.shape[3]
    nb = tile_pairs.shape[0]
    stations = nbl * n
    half = TILE * TILE // ndir
    kall = ndir * kl
    nown = nbl * ndir
    vmem = pl.BlockSpec(memory_space=pltpu.VMEM)
    smem = pl.BlockSpec(memory_space=pltpu.SMEM)
    hbm = pl.BlockSpec(memory_space=pl.ANY)
    dma = pltpu.SemaphoreType.DMA
    out = jax.ShapeDtypeStruct((2, kl, 1, n), F32)
    ngroup = half // GROUP
    gain, dual = pl.pallas_call(
        functools.partial(kernel, nchan, nbl, ndir, poly_coefficients(nchan)),
        out_shape=(out, out),
        in_specs=[hbm, hbm, hbm, hbm, smem, hbm, hbm, hbm],
        out_specs=(vmem, vmem),
        scratch_shapes=[
            pltpu.VMEM((ndir, 2, kl, nb, half), BF16),
            pltpu.VMEM((2, nb, half), BF16),
            pltpu.VMEM((ndir, 2, kl, nb, half), F32),
            pltpu.VMEM((2, nb, half), F32),
            pltpu.VMEM((2, kl, 1, n), F32),
            pltpu.VMEM((2, kl, 1, n), F32),
            pltpu.VMEM((2, nb), jnp.int32),
            pltpu.VMEM((1, nb), jnp.int32),
            pltpu.VMEM((1, stations), jnp.int32),
            pltpu.VMEM((ITERS, nbl, ndir, 2, PAD, n), F32),
            pltpu.VMEM((ITERS + 1, nchan, 2, PAD, n), F32),
            pltpu.VMEM((ITERS, nbl, ndir, 3, PAD, n), F32),
            pltpu.VMEM((ITERS, nbl, ndir, 3, PAD, n), F32),
            pltpu.VMEM((2, PAD, n), F32),
            pltpu.VMEM((GROUP, GROUP), BF16),
            pltpu.VMEM((LANES, ngroup * LANES), BF16),
            pltpu.VMEM((LANES, GROUP), BF16),
            pltpu.VMEM((2 * ngroup * LANES, LANES), BF16),
            pltpu.VMEM((2 * LANES, stations), BF16),
            pltpu.VMEM((nb, stations), F32),
            pltpu.VMEM((PAD, stations), F32),
            pltpu.VMEM((LANES, 2 * stations), BF16),
            pltpu.VMEM((2 * nb, LANES), BF16),
            pltpu.VMEM((2 * kall * nb, ngroup * LANES), F32),
            pltpu.VMEM((2 * kall * nb, GROUP), F32),
            pltpu.VMEM((kall, 2, FOLD, PAD, LANES), F32),
            pltpu.VMEM((3 * kall * nb, ngroup * LANES), F32),
            pltpu.VMEM((nb, LANES), F32),
            pltpu.VMEM((nb, LANES), F32),
            pltpu.VMEM((nb, LANES), F32),
            dma((7,)),
            dma((ndir,)),
            dma((ndir,)),
            dma((ITERS, nown)),
            dma((ITERS, nown)),
            dma((ITERS + 1, nchan)),
            dma((ITERS + 1, nchan)),
            dma((ITERS, nown)),
            dma((ITERS, nown)),
        ],
        compiler_params=pltpu.CompilerParams(
            collective_id=0, has_side_effects=True, vmem_limit_bytes=60 * 1024 * 1024
        ),
    )(
        coherency,
        visibility,
        jnp.transpose(gain_start, (0, 2, 1, 3)),
        jnp.transpose(dual_start, (0, 2, 1, 3)),
        penalty,
        tile_pairs.T,
        valid_counts.reshape(1, nb),
        station_order.reshape(1, stations),
    )
    gain, dual = pl.pallas_call(
        hand_over, out_shape=(out, out), in_specs=[vmem, vmem], out_specs=(vmem, vmem)
    )(gain, dual)
    return jnp.transpose(gain, (0, 2, 1, 3)), jnp.transpose(dual, (0, 2, 1, 3))


def solution(mesh):
    sizes = mesh.shape
    return jax.shard_map(
        functools.partial(on_device, sizes["chan"], sizes["bl"], sizes["dir"]),
        mesh=mesh,
        in_specs=(
            P(None, ("grp", "chan"), "bl", None),
            P(None, ("grp", "chan"), "dir", "bl", None),
            P(None, ("grp", "chan"), "dir", "bl"),
            P(None, ("grp", "chan"), "dir", "bl"),
            P(("grp", "dir")),
            P(("grp", "bl"), None),
            P(("grp", "bl")),
            P("grp"),
        ),
        out_specs=(P(None, ("grp", "chan"), "dir", "bl"), P(None, ("grp", "chan"), "dir", "bl")),
        check_vma=False,
    )
```

```python
import functools

import jax
import jax.numpy as jnp
import numpy as np
from jax import lax
from jax.experimental import pallas as pl
from jax.experimental.pallas import tpu as pltpu
from jax.sharding import PartitionSpec as P

TILE = 64
NPOLY = 3
ITERS = 2
LANES = 128
PAD = 8
FOLD = 4
GROUP = FOLD * LANES
MESH = pl.DeviceIdType.MESH
F32 = jnp.float32
BF16 = jnp.bfloat16


def poly_coefficients(channels):
    points = (2.0 * np.arange(channels) + 1.0) / channels - 1.0
    powers = np.stack([points**d for d in range(NPOLY)], axis=1)
    columns = []
    for degree in range(NPOLY):
        own = np.zeros(NPOLY)
        own[degree] = 1.0
        column = powers[:, degree]
        for earlier, earlier_own in columns:
            dot = np.sum(earlier * column)
            column = column - dot * earlier
            own = own - dot * earlier_own
        norm = np.sqrt(np.sum(column * column))
        columns.append((column / norm, own / norm))
    return [[float(c) for c in own] for _, own in columns]


def basis_at(index, channels, coefficients):
    x = (2 * index + 1).astype(F32) * (1.0 / channels) - 1.0
    return [own[0] + x * (own[1] + x * own[2]) for own in coefficients]


def iota(shape, dim):
    return lax.broadcasted_iota(jnp.int32, shape, dim)


def shift_of(size):
    return jnp.int32(size.bit_length() - 1)


def onehot(mask):
    return jnp.where(mask, 1.0, 0.0).astype(BF16)


def two_pieces(values):
    high = values.astype(BF16)
    low = (values - high.astype(F32)).astype(BF16)
    return high, low


def kernel(
    nchan, nbl, ndir, coefficients,
    coh_hbm, vis_hbm, gain_hbm, dual_hbm, pen_ref, pairs_hbm, cnt_hbm, ord_hbm,
    gout_ref, dout_ref,
    cohv, visv, cohp, visp, gain_ref, dual_ref, pairs_ref, cnt_ref, ord_ref,
    gbuf, cbuf, psend, prec, dualp, perm, rowmat, colmat, rmat, imat, amask,
    tilemask, inmat, select, rowexp, colexp, cross, tbuf, rowtile, coltile, limit,
    lsem, hsend, hrecv, gsend, grecv, csend, crecv, psems, precv,
):
    chan = lax.axis_index("chan")
    mb = lax.axis_index("bl")
    md = lax.axis_index("dir")
    mine = mb * ndir + md
    nown = nbl * ndir
    kl = gain_hbm.shape[1]
    n = gain_hbm.shape[3]
    stations = nbl * n
    nb = pairs_hbm.shape[1]
    slots = TILE * TILE
    half = slots // ndir
    rows_half = half // TILE
    assert stations // TILE <= PAD
    kall = ndir * kl
    ngroup = half // GROUP
    rows_group = LANES * FOLD // TILE
    per_row = LANES // rows_group

    def group_peer(offset):
        peer = lax.rem(mine + offset, nown)
        return lax.div(peer, ndir), lax.rem(peer, ndir)

    def chan_peer(offset):
        return lax.rem(chan + offset, nchan)

    def own_half():
        return pl.ds(pl.multiple_of(md * half, half), half)

    barrier = pltpu.get_barrier_semaphore()
    for offset in range(1, nown):
        pb, pd = group_peer(offset)
        pl.semaphore_signal(barrier, inc=1, device_id={"bl": pb, "dir": pd}, device_id_type=MESH)
    for offset in range(1, nchan):
        pl.semaphore_signal(
            barrier, inc=1, device_id={"chan": chan_peer(offset)}, device_id_type=MESH
        )

    small = [
        pltpu.make_async_copy(source, target, lsem.at[2 + index])
        for index, (source, target) in enumerate(
            [
                (gain_hbm, gain_ref),
                (dual_hbm, dual_ref),
                (pairs_hbm, pairs_ref),
                (cnt_hbm, cnt_ref),
                (ord_hbm, ord_ref),
            ]
        )
    ]
    local = [
        pltpu.make_async_copy(coh_hbm.at[:, 0, :, :, own_half()], cohv.at[md], lsem.at[0]),
        pltpu.make_async_copy(vis_hbm.at[:, 0, :, own_half()], visv, lsem.at[1]),
    ]
    for copy in small + local:
        copy.start()

    gbuf[0, mb, md] = jnp.zeros((2, PAD, n), F32)
    dualp[...] = jnp.zeros((2, PAD, n), F32)
    for copy in small[:2]:
        copy.wait()
    for c in range(2):
        for k in range(kl):
            gbuf[0, mb, md, c, k : k + 1, :] = gain_ref[c, k]
            dualp[c, k : k + 1, :] = dual_ref[c, k]
    gain_now = gbuf[0, mb, md]
    dual_now = dualp[...]
    cbuf[0, chan] = gain_now + dual_now

    pl.semaphore_wait(barrier, nown - 1 + nchan - 1)

    halves = []
    for offset in range(1, ndir):
        peer = lax.rem(md + offset, ndir)
        source = lax.rem(md + ndir - offset, ndir)
        copy = pltpu.make_async_remote_copy(
            src_ref=coh_hbm.at[:, 0, :, :, pl.ds(pl.multiple_of(peer * half, half), half)],
            dst_ref=cohv.at[md],
            send_sem=hsend.at[offset],
            recv_sem=hrecv.at[md],
            device_id={"dir": peer},
            device_id_type=MESH,
        )
        arrival = pltpu.make_async_remote_copy(
            src_ref=coh_hbm.at[:, 0, :, :, pl.ds(pl.multiple_of(peer * half, half), half)],
            dst_ref=cohv.at[source],
            send_sem=hsend.at[offset],
            recv_sem=hrecv.at[source],
            device_id={"dir": peer},
            device_id_type=MESH,
        )
        halves.append((copy, arrival))

    def group_copies(source_of, target, send_sem, recv_sem, phase):
        made = []
        for offset in range(1, nown):
            pb, pd = group_peer(offset)
            sb, sd = group_peer(nown - offset)
            common = dict(
                src_ref=source_of(pb, pd),
                send_sem=send_sem.at[phase, offset],
                device_id={"bl": pb, "dir": pd},
                device_id_type=MESH,
            )
            copy = pltpu.make_async_remote_copy(
                dst_ref=target.at[phase, mb, md, :, 0:kl, :], recv_sem=recv_sem.at[phase, mine], **common
            )
            arrival = pltpu.make_async_remote_copy(
                dst_ref=target.at[phase, sb, sd, :, 0:kl, :],
                recv_sem=recv_sem.at[phase, sb * ndir + sd],
                **common,
            )
            made.append((copy, arrival))
        return made

    def gain_copies(phase):
        return group_copies(
            lambda pb, pd: gbuf.at[phase, mb, md, :, 0:kl, :], gbuf, gsend, grecv, phase
        )

    def term_copies(phase):
        return group_copies(
            lambda pb, pd: psend.at[phase, pb, pd, :, 0:kl, :], prec, psems, precv, phase
        )

    def chan_copies(phase):
        made = []
        for offset in range(1, nchan):
            peer = chan_peer(offset)
            source = chan_peer(nchan - offset)
            common = dict(
                src_ref=cbuf.at[phase, chan, :, 0:kl, :],
                send_sem=csend.at[phase, offset],
                device_id={"chan": peer},
                device_id_type=MESH,
            )
            copy = pltpu.make_async_remote_copy(
                dst_ref=cbuf.at[phase, chan, :, 0:kl, :], recv_sem=crecv.at[phase, chan], **common
            )
            arrival = pltpu.make_async_remote_copy(
                dst_ref=cbuf.at[phase, source, :, 0:kl, :], recv_sem=crecv.at[phase, source], **common
            )
            made.append((copy, arrival))
        return made

    def start(copies):
        for copy, _ in copies:
            copy.start()

    def arrive(copies):
        for _, arrival in copies:
            arrival.wait_recv()

    def finish(copies):
        for copy, _ in copies:
            copy.wait_send()

    everything = []
    gains = gain_copies(0)
    start(gains)
    start(halves)
    sums = chan_copies(0)
    start(sums)
    everything += [gains, halves, sums]

    psend[...] = jnp.zeros(psend.shape, F32)
    for copy in small[2:]:
        copy.wait()
    order = ord_ref[...]
    within = jnp.bitwise_and(order, TILE - 1)
    tile_of = lax.shift_right_logical(order, shift_of(TILE))
    tilemask[...] = jnp.where(iota((PAD, stations), 0) == tile_of, 1.0, 0.0)
    both = iota((LANES, stations), 0)
    inmat[:, 0:stations] = onehot(both == within)
    inmat[:, stations : 2 * stations] = onehot(both - TILE == within)
    to_lane = iota((1, GROUP), 1)
    lane_row = lax.shift_right_logical(jnp.bitwise_and(to_lane, LANES - 1), shift_of(per_row))
    lane_col = lax.shift_right_logical(to_lane, shift_of(LANES)) * per_row + jnp.bitwise_and(
        to_lane, per_row - 1
    )
    perm[...] = onehot(iota((GROUP, GROUP), 0) == lane_row * TILE + lane_col)
    piece_row = jnp.bitwise_and(iota((LANES, GROUP), 0), TILE - 1)
    colmat[...] = onehot(piece_row == lane_col)
    shape = (LANES, ngroup * LANES)
    lane_row = lax.shift_right_logical(iota((1, ngroup * LANES), 1), shift_of(per_row))
    piece_row = jnp.bitwise_and(iota(shape, 0), TILE - 1)
    rowmat[...] = onehot(piece_row == md * rows_half + lane_row)
    shape = (ngroup * LANES, LANES)
    summing = onehot(lax.shift_right_logical(iota(shape, 0), shift_of(per_row)) == iota(shape, 1))
    rmat[0 : ngroup * LANES, :] = summing
    rmat[ngroup * LANES :, :] = summing
    row_in = iota((LANES, stations), 0)
    placing = onehot((row_in < rows_half) & (row_in + md * rows_half == within))
    imat[0:LANES, :] = placing
    imat[LANES : 2 * LANES, :] = placing

    def column(row):
        square = jnp.where(iota((nb, nb), 0) == iota((nb, nb), 1), row.astype(F32), 0.0)
        return jnp.sum(square, axis=1, keepdims=True)

    row_column = column(pairs_ref[0:1, :])
    rowtile[...] = jnp.broadcast_to(row_column, (nb, LANES))
    coltile[...] = jnp.broadcast_to(column(pairs_ref[1:2, :]), (nb, LANES))
    limit[...] = jnp.broadcast_to(column(cnt_ref[...]), (nb, LANES))
    amask[...] = jnp.where(tile_of.astype(F32) == row_column, 1.0, 0.0)
    lane_tile = iota((nb, LANES), 1).astype(F32)
    select[0:nb, :] = onehot(rowtile[...] == lane_tile)
    select[nb : 2 * nb, :] = onehot(coltile[...] == lane_tile)

    row_k = iota((PAD, n), 0)
    stiffness = jnp.ones((PAD, n), F32)
    for k in range(kl):
        stiffness = jnp.where(row_k == k, pen_ref[k], stiffness)

    def spread_gains(phase):
        highs, lows = [], []
        for d in range(ndir):
            for c in range(2):
                held = jnp.concatenate([gbuf[phase, b, d, c] for b in range(nbl)], axis=1)
                first = held.astype(BF16).astype(F32)
                second = held - first
                for k in range(kl):
                    highs.append(first[k : k + 1, :] * tilemask[...])
                    lows.append(second[k : k + 1, :] * tilemask[...])
        pieces = jnp.concatenate(
            [jnp.concatenate(highs, axis=0), jnp.concatenate(lows, axis=0)], axis=1
        ).astype(BF16)
        natural = lax.dot_general(
            pieces, inmat[...], (((1,), (1,)), ((), ())), preferred_element_type=F32
        )
        by_tile = jnp.concatenate(
            [natural[i * PAD : (i + 1) * PAD, :] for i in range(2 * kall)], axis=1
        )
        by_tile = jnp.concatenate([by_tile, jnp.zeros_like(by_tile)], axis=0).astype(BF16)
        chosen = jnp.dot(
            select[:, 0 : 2 * PAD], by_tile, preferred_element_type=F32
        ).astype(BF16)
        for first, table, target in ((0, rowmat, rowexp), (nb, colmat, colexp)):
            stacked = jnp.concatenate(
                [
                    chosen[first : first + nb, i * LANES : (i + 1) * LANES]
                    for i in range(2 * kall)
                ],
                axis=0,
            )
            target[...] = jnp.dot(stacked, table[...], preferred_element_type=F32)

    def valid_slots(g):
        lane = iota((nb, GROUP), 1)
        in_lane = jnp.bitwise_and(lane, LANES - 1)
        row = md * rows_half + g * rows_group + lax.shift_right_logical(in_lane, shift_of(per_row))
        col = lax.shift_right_logical(lane, shift_of(LANES)) * per_row + jnp.bitwise_and(
            lane, per_row - 1
        )

        def across(table):
            return jnp.concatenate([table[...]] * FOLD, axis=1)

        inside = (row * TILE + col).astype(F32) < across(limit)
        same = across(rowtile) == across(coltile)
        return jnp.where(inside & jnp.logical_not(same & (row == col)), 1.0, 0.0)

    def permute_half(d):
        def step(g, carry):
            lanes = pl.ds(pl.multiple_of(g * GROUP, GROUP), GROUP)
            source = cohv[d, :, :, :, lanes].reshape(2 * kl * nb, GROUP)
            moved = jnp.dot(source, perm[...], preferred_element_type=F32)
            moved = moved.reshape(2, kl, nb, GROUP)
            cohp[d, :, :, :, lanes] = moved * valid_slots(g)[None, None]
            return carry

        lax.fori_loop(0, ngroup, step, 0, unroll=True)

    def permute_vis():
        def step(g, carry):
            lanes = pl.ds(pl.multiple_of(g * GROUP, GROUP), GROUP)
            source = visv[:, :, lanes].reshape(2 * nb, GROUP)
            moved = jnp.dot(source, perm[...], preferred_element_type=F32)
            visp[:, :, lanes] = moved.reshape(2, nb, GROUP)
            return carry

        lax.fori_loop(0, ngroup, step, 0, unroll=True)

    def station_terms(phase):
        def tile_step(step, carry):
            g = step // (nb // PAD)
            part = lax.rem(step, nb // PAD)
            lanes = pl.ds(pl.multiple_of(g * LANES, LANES), LANES)
            blocks = pl.ds(pl.multiple_of(part * PAD, PAD), PAD)

            def at(index):
                return pl.ds(pl.multiple_of(index * nb + part * PAD, PAD), PAD)

            residuals = []
            for v in range(FOLD):
                here = pl.ds(pl.multiple_of(g * GROUP + v * LANES, LANES), LANES)
                cols = slice(v * LANES, (v + 1) * LANES)
                model_r = jnp.zeros((PAD, LANES), F32)
                model_i = jnp.zeros((PAD, LANES), F32)
                for d in range(ndir):
                    for k in range(kl):
                        re, im = d * 2 * kl + k, d * 2 * kl + kl + k
                        coh_r = cohp[d, 0, k, blocks, here]
                        coh_i = cohp[d, 1, k, blocks, here]
                        col_r, col_i = colexp[at(re), cols], colexp[at(im), cols]
                        cr = coh_r * col_r + coh_i * col_i
                        ci = coh_i * col_r - coh_r * col_i
                        cross[d * kl + k, 0, v] = cr
                        cross[d * kl + k, 1, v] = ci
                        row_r, row_i = rowexp[at(re), lanes], rowexp[at(im), lanes]
                        model_r = model_r + (row_r * cr - row_i * ci)
                        model_i = model_i + (row_r * ci + row_i * cr)
                res_r = visp[0, blocks, here] - model_r
                res_i = visp[1, blocks, here] - model_i
                residuals.append((res_r, res_i))
            for index in range(kall):
                numer_r = numer_i = weight = None
                for v, (res_r, res_i) in enumerate(residuals):
                    cr, ci = cross[index, 0, v], cross[index, 1, v]
                    parts = (
                        res_r * cr + res_i * ci,
                        res_i * cr - res_r * ci,
                        cr * cr + ci * ci,
                    )
                    if numer_r is None:
                        numer_r, numer_i, weight = parts
                    else:
                        numer_r = numer_r + parts[0]
                        numer_i = numer_i + parts[1]
                        weight = weight + parts[2]
                tbuf[at(index), lanes] = numer_r
                tbuf[at(kall + index), lanes] = numer_i
                tbuf[at(2 * kall + index), lanes] = weight
            return carry

        lax.fori_loop(0, ngroup * (nb // PAD), tile_step, 0, unroll=4)

        high, low = two_pieces(tbuf[...])
        by_block = jnp.dot(
            jnp.concatenate([high, low], axis=1), rmat[...], preferred_element_type=F32
        )
        high, low = two_pieces(by_block)
        placed = jnp.dot(
            jnp.concatenate([high, low], axis=1), imat[...], preferred_element_type=F32
        )
        kept = placed.reshape(3 * kall, nb, stations) * amask[...][None]
        summed = jnp.sum(kept, axis=1)
        for q in range(3):
            for d in range(ndir):
                at = (q * ndir + d) * kl
                for b in range(nbl):
                    psend[phase, b, d, q, 0:kl, :] = summed[at : at + kl, b * n : (b + 1) * n]

    mine_basis = basis_at(chan, nchan, coefficients)

    def center_of(phase):
        total = jnp.zeros((2, PAD, n), F32)
        for offset in range(nchan):
            source = chan_peer(offset)
            theirs = basis_at(source, nchan, coefficients)
            scale = sum(a * b for a, b in zip(mine_basis, theirs))
            total = total + scale * cbuf[phase, source]
        return total

    for iteration in range(ITERS):
        if iteration == 0:
            for copy in local:
                copy.wait()
            permute_half(md)
            permute_vis()
            arrive(halves)
            for offset in range(1, ndir):
                permute_half(lax.rem(md + offset, ndir))
        arrive(gains)
        spread_gains(iteration)
        station_terms(iteration)
        moved = term_copies(iteration)
        start(moved)
        everything.append(moved)
        arrive(sums)
        center = center_of(iteration)
        if iteration > 0:
            dual_now = dual_now + gain_now - center
        target = center - dual_now
        arrive(moved)
        terms = psend[iteration, mb, md]
        for offset in range(1, nown):
            sb, sd = group_peer(offset)
            terms = terms + prec[iteration, sb, sd]
        weight = terms[2]
        denominator = weight + stiffness
        gain_now = jnp.stack(
            [
                (terms[c] + gain_now[c] * weight + stiffness * target[c]) / denominator
                for c in range(2)
            ]
        )
        if iteration + 1 < ITERS:
            gbuf[iteration + 1, mb, md] = gain_now
            gains = gain_copies(iteration + 1)
            start(gains)
            everything.append(gains)
        cbuf[iteration + 1, chan] = gain_now + dual_now
        sums = chan_copies(iteration + 1)
        start(sums)
        everything.append(sums)
    for c in range(2):
        for k in range(kl):
            gout_ref[c, k] = gain_now[c, k : k + 1, :]
    arrive(sums)
    center = center_of(ITERS)
    dual_now = dual_now + gain_now - center
    for c in range(2):
        for k in range(kl):
            dout_ref[c, k] = dual_now[c, k : k + 1, :]
    for copies in everything:
        finish(copies)


def hand_over(gain_ref, dual_ref, gout_ref, dout_ref):
    gout_ref[...] = gain_ref[...]
    dout_ref[...] = dual_ref[...]


def on_device(
    nchan, nbl, ndir,
    visibility, coherency, gain_start, dual_start, penalty, tile_pairs, valid_counts, station_order,
):
    kl = gain_start.shape[2]
    n = gain_start.shape[3]
    nb = tile_pairs.shape[0]
    stations = nbl * n
    half = TILE * TILE // ndir
    kall = ndir * kl
    nown = nbl * ndir
    vmem = pl.BlockSpec(memory_space=pltpu.VMEM)
    smem = pl.BlockSpec(memory_space=pltpu.SMEM)
    hbm = pl.BlockSpec(memory_space=pl.ANY)
    dma = pltpu.SemaphoreType.DMA
    out = jax.ShapeDtypeStruct((2, kl, 1, n), F32)
    ngroup = half // GROUP
    gain, dual = pl.pallas_call(
        functools.partial(kernel, nchan, nbl, ndir, poly_coefficients(nchan)),
        out_shape=(out, out),
        in_specs=[hbm, hbm, hbm, hbm, smem, hbm, hbm, hbm],
        out_specs=(vmem, vmem),
        scratch_shapes=[
            pltpu.VMEM((ndir, 2, kl, nb, half), BF16),
            pltpu.VMEM((2, nb, half), BF16),
            pltpu.VMEM((ndir, 2, kl, nb, half), F32),
            pltpu.VMEM((2, nb, half), F32),
            pltpu.VMEM((2, kl, 1, n), F32),
            pltpu.VMEM((2, kl, 1, n), F32),
            pltpu.VMEM((2, nb), jnp.int32),
            pltpu.VMEM((1, nb), jnp.int32),
            pltpu.VMEM((1, stations), jnp.int32),
            pltpu.VMEM((ITERS, nbl, ndir, 2, PAD, n), F32),
            pltpu.VMEM((ITERS + 1, nchan, 2, PAD, n), F32),
            pltpu.VMEM((ITERS, nbl, ndir, 3, PAD, n), F32),
            pltpu.VMEM((ITERS, nbl, ndir, 3, PAD, n), F32),
            pltpu.VMEM((2, PAD, n), F32),
            pltpu.VMEM((GROUP, GROUP), BF16),
            pltpu.VMEM((LANES, ngroup * LANES), BF16),
            pltpu.VMEM((LANES, GROUP), BF16),
            pltpu.VMEM((2 * ngroup * LANES, LANES), BF16),
            pltpu.VMEM((2 * LANES, stations), BF16),
            pltpu.VMEM((nb, stations), F32),
            pltpu.VMEM((PAD, stations), F32),
            pltpu.VMEM((LANES, 2 * stations), BF16),
            pltpu.VMEM((2 * nb, LANES), BF16),
            pltpu.VMEM((2 * kall * nb, ngroup * LANES), F32),
            pltpu.VMEM((2 * kall * nb, GROUP), F32),
            pltpu.VMEM((kall, 2, FOLD, PAD, LANES), F32),
            pltpu.VMEM((3 * kall * nb, ngroup * LANES), F32),
            pltpu.VMEM((nb, LANES), F32),
            pltpu.VMEM((nb, LANES), F32),
            pltpu.VMEM((nb, LANES), F32),
            dma((7,)),
            dma((ndir,)),
            dma((ndir,)),
            dma((ITERS, nown)),
            dma((ITERS, nown)),
            dma((ITERS + 1, nchan)),
            dma((ITERS + 1, nchan)),
            dma((ITERS, nown)),
            dma((ITERS, nown)),
        ],
        compiler_params=pltpu.CompilerParams(
            collective_id=0, has_side_effects=True, vmem_limit_bytes=60 * 1024 * 1024
        ),
    )(
        coherency,
        visibility,
        jnp.transpose(gain_start, (0, 2, 1, 3)),
        jnp.transpose(dual_start, (0, 2, 1, 3)),
        penalty,
        tile_pairs.T,
        valid_counts.reshape(1, nb),
        station_order.reshape(1, stations),
    )
    gain, dual = pl.pallas_call(
        hand_over, out_shape=(out, out), in_specs=[vmem, vmem], out_specs=(vmem, vmem)
    )(gain, dual)
    return jnp.transpose(gain, (0, 2, 1, 3)), jnp.transpose(dual, (0, 2, 1, 3))


def solution(mesh):
    sizes = mesh.shape
    return jax.shard_map(
        functools.partial(on_device, sizes["chan"], sizes["bl"], sizes["dir"]),
        mesh=mesh,
        in_specs=(
            P(None, ("grp", "chan"), "bl", None),
            P(None, ("grp", "chan"), "dir", "bl", None),
            P(None, ("grp", "chan"), "dir", "bl"),
            P(None, ("grp", "chan"), "dir", "bl"),
            P(("grp", "dir")),
            P(("grp", "bl"), None),
            P(("grp", "bl")),
            P("grp"),
        ),
        out_specs=(P(None, ("grp", "chan"), "dir", "bl"), P(None, ("grp", "chan"), "dir", "bl")),
        check_vma=False,
    )
```
